256 devices in a mesh: dp: 8 (over y, core), tower: 2 (over x_lo), seq: 16 (over x_hi, z).
Axes of the slice: x: 4 (x_hi: 2, x_lo: 2; x = x_hi * 2 + x_lo), y: 4, z: 8, core: 2. Of those that a mesh axis runs over, the one named last changes fastest.
Arguments:
- query_proj: bfloat16 [8, 2, 2048, 1536], P('dp', 'tower', 'seq'), may hold values from -90 to 90
- key_proj: bfloat16 [8, 2, 2048, 1536], P('dp', 'tower', 'seq'), may hold values from -9 to 9
- value_proj: bfloat16 [8, 2, 2048, 1536], P('dp', 'tower', 'seq'), may hold values from -6 to 6
- out_grad: bfloat16 [8, 2, 2048, 1536], P('dp', 'tower', 'seq'), may hold values from -6 to 6
- gate_scale: float32 [2, 1536], P('tower'), may hold values from 2 to 16
Outputs:
- attended: bfloat16 [8, 2, 2048, 1536], P('dp', 'tower', 'seq')
- query_grad: bfloat16 [8, 2, 2048, 1536], P('dp', 'tower', 'seq')
- key_grad: bfloat16 [8, 2, 2048, 1536], P('dp', 'tower', 'seq')
- value_grad: bfloat16 [8, 2, 2048, 1536], P('dp', 'tower', 'seq')
- gate_grad: float32 [2, 1536], P('tower')
The draws below stay inside these ranges and needn't reach their ends.
All inputs are finite; a program needn't handle non-finite values.
Results may differ from the reference program's by a relative error of at most 0.035.
Values may be sent and summed in bfloat16 or wider, within the bound.
A program may use at most 128 MiB of HBM per device.

```python
import math
import jax
import jax.numpy as jnp
from jax import lax

HEADS = 12
HEAD_DIM = 128
ROWS = 128
D = 1536
TOKENS = 2048
CLIPS = 8
TOWERS = 2


def key_field(key):
    normal_field = jax.random.normal(jax.random.fold_in(key, 7), (CLIPS, TOWERS, TOKENS, D), jnp.float32)
    return 1.4 * jnp.clip(normal_field, -6.0, 6.0)


def draw_key_proj(key, part):
    field = key_field(key)
    return field.astype(jnp.bfloat16)


def draw_query_proj(key, part):
    key = jax.random.fold_in(key, 3)
    normal_field = jax.random.normal(key, (CLIPS, TOWERS, TOKENS, D), jnp.float32)
    field = 1.4 * jnp.clip(normal_field, -6.0, 6.0)
    return field.astype(jnp.bfloat16)


def steps_of(rng, shape, cuts, least, top_value):
    loudness = 1.0
    for dim, blocks in cuts:
        steps = jax.random.uniform(jax.random.fold_in(jax.random.fold_in(rng, 6), dim), (blocks,), jnp.float32, least / len(cuts), top_value / len(cuts))
        loudness = loudness * jnp.repeat(jnp.exp(steps), shape[dim] // blocks).reshape((-1,) + (1,) * (len(shape) - 1 - dim))
    return loudness


def scatter_about(key, dims, width, most, cuts=(), dtype=jnp.bfloat16):
    values = width * jax.random.normal(key, dims, jnp.float32)
    if cuts:
        values = values * steps_of(key, dims, cuts, -0.22, 0.18)
    return jnp.clip(values, -most, most).astype(dtype)


def setup_inputs(seed: int = 0) -> dict:
    arg_keys = jax.random.split(jax.random.key(seed), 6)
    return {
        "query_proj": draw_query_proj(jax.random.fold_in(arg_keys[5], 71), 0),
        "key_proj": draw_key_proj(jax.random.fold_in(arg_keys[5], 71), 0),
        "value_proj": scatter_about(arg_keys[2], (CLIPS, TOWERS, TOKENS, D), 1.0, 6.0, ((0, 8), (1, 2), (2, 16))),
        "out_grad": scatter_about(arg_keys[3], (CLIPS, TOWERS, TOKENS, D), 1.0, 6.0, ((0, 8), (1, 2), (2, 16))),
        "gate_scale": jnp.clip(jnp.exp(math.log(16.0) - 2.0794415 * jax.random.uniform(arg_keys[4], (TOWERS, D), jnp.float32) ** steps_of(arg_keys[4], (TOWERS, D), ((0, 2),), -0.2, 0.2)), 2.0, 16.0),
    }


def one_pair(queries_in, keys_in, values_in, cotangent_in, gate_row):
    token_count = queries_in.shape[0]
    score_scale = 1.0 / math.sqrt(HEAD_DIM)
    query_heads = queries_in.astype(jnp.float32).reshape(token_count, HEADS, HEAD_DIM)
    key_heads = keys_in.astype(jnp.float32).reshape(token_count, HEADS, HEAD_DIM)
    value_heads = values_in.astype(jnp.float32).reshape(token_count, HEADS, HEAD_DIM)
    scores = jnp.einsum('ihd,jhd->hij', query_heads, key_heads) * score_scale
    row_top = lax.optimization_barrier(jnp.max(scores, axis=-1, keepdims=True))
    weights = jnp.exp(scores - row_top)
    probs = weights / lax.optimization_barrier(jnp.sum(weights, axis=-1, keepdims=True))
    probs_low = probs.astype(jnp.bfloat16)
    probs_back = probs_low.astype(jnp.float32)
    mixed = jnp.einsum('hij,jhd->ihd', probs_back, value_heads).reshape(token_count, D)
    attended = (gate_row * mixed).astype(jnp.bfloat16)
    cotangent_wide = cotangent_in.astype(jnp.float32)
    grad_heads = (gate_row * cotangent_wide).astype(jnp.bfloat16)
    gate_term = lax.optimization_barrier(jnp.sum(cotangent_wide * mixed, axis=0))
    grad_wide = grad_heads.astype(jnp.float32).reshape(token_count, HEADS, HEAD_DIM)
    delta = lax.optimization_barrier(jnp.sum(grad_wide * mixed.reshape(token_count, HEADS, HEAD_DIM), axis=-1)).T
    grad_probs = jnp.einsum('ihd,jhd->hij', grad_wide, value_heads)
    grad_scores = (probs * (grad_probs - delta[:, :, None]) * score_scale).astype(jnp.bfloat16)
    score_back = grad_scores.astype(jnp.float32)
    query_grad = jnp.einsum('hij,jhd->ihd', score_back, key_heads).reshape(token_count, D).astype(jnp.bfloat16)
    block_count = token_count // ROWS
    score_blocks = score_back.reshape(HEADS, block_count, ROWS, token_count)
    prob_blocks = probs_back.reshape(HEADS, block_count, ROWS, token_count)
    query_blocks = query_heads.reshape(block_count, ROWS, HEADS, HEAD_DIM)
    grad_blocks = grad_wide.reshape(block_count, ROWS, HEADS, HEAD_DIM)
    key_partial = jnp.einsum('hbij,bihd->bjhd', score_blocks, query_blocks).astype(jnp.bfloat16)
    value_partial = jnp.einsum('hbij,bihd->bjhd', prob_blocks, grad_blocks).astype(jnp.bfloat16)
    key_partial = lax.optimization_barrier(key_partial)
    value_partial = lax.optimization_barrier(value_partial)
    key_grad = lax.optimization_barrier(jnp.sum(key_partial.astype(jnp.float32), axis=0)).reshape(token_count, D).astype(jnp.bfloat16)
    value_grad = lax.optimization_barrier(jnp.sum(value_partial.astype(jnp.float32), axis=0)).reshape(token_count, D).astype(jnp.bfloat16)
    return (attended, query_grad, key_grad, value_grad, gate_term)

def reference(query_proj, key_proj, value_proj, out_grad, gate_scale):
    pair_count = CLIPS * TOWERS
    other_keys = key_proj[:, ::-1]
    other_values = value_proj[:, ::-1]
    gate_rows = jnp.broadcast_to(gate_scale[None], (CLIPS, TOWERS, D))
    flat_inputs = (query_proj.reshape(pair_count, TOKENS, D), other_keys.reshape(pair_count, TOKENS, D), other_values.reshape(pair_count, TOKENS, D), out_grad.reshape(pair_count, TOKENS, D), gate_rows.reshape(pair_count, D))
    results = lax.map(lambda packed: one_pair(*packed), flat_inputs)
    attended = results[0].reshape(CLIPS, TOWERS, TOKENS, D)
    query_grad = results[1].reshape(CLIPS, TOWERS, TOKENS, D)
    key_grad = results[2].reshape(CLIPS, TOWERS, TOKENS, D)[:, ::-1]
    value_grad = results[3].reshape(CLIPS, TOWERS, TOKENS, D)[:, ::-1]
    gate_grad = lax.optimization_barrier(jnp.sum(results[4].reshape(CLIPS, TOWERS, D), axis=0))
    return (attended, query_grad, key_grad, value_grad, gate_grad)
```

```python
import math

import jax
import jax.numpy as jnp
from jax import lax
from jax.experimental import pallas as pl
from jax.experimental.pallas import tpu as pltpu
from jax.sharding import PartitionSpec as P

HEADS = 12
HEAD_DIM = 128
ROWS = 128
BLOCKS = 16
TOKENS = ROWS * BLOCKS
D = HEADS * HEAD_DIM
Z = 8
CLIPS = 8
CHUNK = 256
CHUNKS = TOKENS // CHUNK
PER_CHUNK = CHUNK // ROWS
SCALE = 1.0 / math.sqrt(HEAD_DIM)
EXP2_SCALE = SCALE * math.log2(math.e)
MESH = pl.DeviceIdType.MESH


def place_of(tower, x_hi, slot, core):
    ring = (slot // 3) * 4 + slot % 3 + 1
    z = (ring + 2 * x_hi + tower + 16 - 2 * core) % Z
    return x_hi * Z + z


def rows_of(block):
    return pl.ds(pl.multiple_of(block * ROWS, ROWS), ROWS)


def lanes_of(head):
    return pl.ds(pl.multiple_of(head * HEAD_DIM, HEAD_DIM), HEAD_DIM)


def kernel(
    query_ref,
    key_ref,
    value_ref,
    cot_ref,
    gate_ref,
    att_ref,
    dq_ref,
    dk_ref,
    dv_ref,
    gate_grad_ref,
    q_all,
    k_all,
    v_all,
    g_all,
    att_all,
    dq_all,
    dk_acc,
    dv_acc,
    dk_all,
    dv_all,
    gate_acc,
    gate_in,
    gate_total,
    gate_heads,
    kv_send,
    qg_send,
    k_recv,
    v_recv,
    q_recv,
    g_recv,
    rows_send,
    cols_send,
    out_recv,
    clip_send,
    clip_recv,
    head_send,
    head_recv,
):
    clip = lax.axis_index("dp")
    tower = lax.axis_index("tower")
    seq = lax.axis_index("seq")
    core = clip % 2
    x_hi = seq // Z
    z = seq % Z
    ring = (z + 2 * core + 16 - 2 * x_hi - tower) % Z
    has_unit = ring % 4 != 0
    slot = (ring // 4) * 3 + lax.max(ring % 4 - 1, 0)
    head = x_hi * 6 + slot

    def device(clip_to, tower_to, seq_to):
        return {"dp": clip_to, "tower": tower_to, "seq": seq_to}

    def peer_clip(step):
        other = (clip + step) % CLIPS
        other_z = (z + 2 * core + 16 - 2 * (other % 2)) % Z
        return other, x_hi * Z + other_z

    barrier = pltpu.get_barrier_semaphore()

    def greet(step, carry):
        place = (tower * BLOCKS + seq + step) % (2 * BLOCKS)
        pl.semaphore_signal(
            barrier,
            inc=1,
            device_id=device(clip, place // BLOCKS, place % BLOCKS),
            device_id_type=MESH,
        )
        return carry

    lax.fori_loop(1, 2 * BLOCKS, greet, 0)

    def greet_clip(step, carry):
        other, place = peer_clip(step)
        pl.semaphore_signal(
            barrier, inc=1, device_id=device(other, tower, place), device_id_type=MESH
        )
        return carry

    lax.fori_loop(1, CLIPS, greet_clip, 0)
    pl.semaphore_wait(barrier, 2 * BLOCKS - 1 + CLIPS - 1)

    def target(step, tower_to):
        half = step // 2
        to_x = (x_hi + step) % 2
        turn = (half // 2) * (1 - 2 * (half % 2)) + 5 * (half % 2)
        to_ring = (z + 2 * core + 16 - 2 * to_x - tower_to) % Z
        to_slot = ((to_ring * 3) // 4 + turn) % 6
        return to_x * 6 + to_slot, place_of(tower_to, to_x, to_slot, core)

    def send_kv(step, carry):
        to_head, place = target(step, 1 - tower)
        for index, (source, sink, arrived) in enumerate(
            ((key_ref, k_all, k_recv), (value_ref, v_all, v_recv))
        ):
            pltpu.make_async_remote_copy(
                src_ref=source.at[0, 0, :, lanes_of(to_head)],
                dst_ref=sink.at[rows_of(seq)],
                send_sem=kv_send.at[index, to_head],
                recv_sem=arrived.at[seq],
                device_id=device(clip, 1 - tower, place),
                device_id_type=MESH,
            ).start()
        return carry

    lax.fori_loop(0, HEADS, send_kv, 0)

    def query_copy(index, to_head, place):
        source, sink, arrived = ((query_ref, q_all, q_recv), (cot_ref, g_all, g_recv))[index]
        return pltpu.make_async_remote_copy(
            src_ref=source.at[0, 0, :, lanes_of(to_head)],
            dst_ref=sink.at[rows_of(seq)],
            send_sem=qg_send.at[index, to_head],
            recv_sem=arrived.at[seq],
            device_id=device(clip, tower, place),
            device_id_type=MESH,
        )

    def send_qg(step, carry):
        to_head, place = target(step, tower)

        @pl.when(place != seq)
        def _():
            for index in range(2):
                query_copy(index, to_head, place).start()

        @pl.when(place == seq)
        def _():
            for source, sink, arrived in ((query_ref, q_all, q_recv), (cot_ref, g_all, g_recv)):
                pltpu.make_async_copy(
                    source.at[0, 0, :, lanes_of(to_head)],
                    sink.at[rows_of(seq)],
                    arrived.at[seq],
                ).start()

        return carry

    lax.fori_loop(0, HEADS, send_qg, 0)

    def row_copy(index, block):
        source, sink = ((att_all, att_ref), (dq_all, dq_ref))[index]
        return pltpu.make_async_remote_copy(
            src_ref=source.at[rows_of(block)],
            dst_ref=sink.at[0, 0, :, lanes_of(head)],
            send_sem=rows_send.at[index, block],
            recv_sem=out_recv.at[index, head],
            device_id=device(clip, tower, block),
            device_id_type=MESH,
        )

    def column_copy(index, block):
        source, sink = ((dk_all, dk_ref), (dv_all, dv_ref))[index]
        return pltpu.make_async_remote_copy(
            src_ref=source.at[rows_of(block)],
            dst_ref=sink.at[0, 0, :, lanes_of(head)],
            send_sem=cols_send.at[index, block],
            recv_sem=out_recv.at[2 + index, head],
            device_id=device(clip, 1 - tower, block),
            device_id_type=MESH,
        )

    def clip_copy(step):
        other, place = peer_clip(step)
        return pltpu.make_async_remote_copy(
            src_ref=gate_acc,
            dst_ref=gate_in.at[clip],
            send_sem=clip_send.at[step],
            recv_sem=clip_recv.at[clip],
            device_id=device(other, tower, place),
            device_id_type=MESH,
        )

    def head_copy(step):
        place = (seq + step) % BLOCKS
        return pltpu.make_async_remote_copy(
            src_ref=gate_total,
            dst_ref=gate_heads.at[head],
            send_sem=head_send.at[step],
            recv_sem=head_recv.at[head],
            device_id=device(clip, tower, place),
            device_id_type=MESH,
        )

    @pl.when(has_unit)
    def _():
        gate_row = gate_ref[:, lanes_of(head)]
        gate_acc[...] = jnp.zeros_like(gate_acc)
        dk_acc[...] = jnp.zeros_like(dk_acc)
        dv_acc[...] = jnp.zeros_like(dv_acc)

        def wait_kv(block, carry):
            pltpu.make_async_copy(
                k_all.at[rows_of(block)], k_all.at[rows_of(block)], k_recv.at[block]
            ).wait()
            pltpu.make_async_copy(
                v_all.at[rows_of(block)], v_all.at[rows_of(block)], v_recv.at[block]
            ).wait()
            return carry

        lax.fori_loop(0, BLOCKS, wait_kv, 0)

        def one_chunk(step, carry):
            chunk = (seq // PER_CHUNK + step) % CHUNKS
            for part in range(PER_CHUNK):
                block = chunk * PER_CHUNK + part
                pltpu.make_async_copy(
                    q_all.at[rows_of(block)], q_all.at[rows_of(block)], q_recv.at[block]
                ).wait()
                pltpu.make_async_copy(
                    g_all.at[rows_of(block)], g_all.at[rows_of(block)], g_recv.at[block]
                ).wait()
            rows = pl.ds(pl.multiple_of(chunk * CHUNK, CHUNK), CHUNK)
            queries = q_all[rows, :]
            keys = k_all[...]
            values = v_all[...]
            cot = g_all[rows, :].astype(jnp.float32)
            grad_heads = (gate_row * cot).astype(jnp.bfloat16)
            scores = lax.dot_general(
                queries, keys, (((1,), (1,)), ((), ())), preferred_element_type=jnp.float32
            )
            row_top = jnp.max(scores, axis=-1, keepdims=True)
            weights = jnp.exp2((scores - row_top) * EXP2_SCALE)
            mass = jnp.sum(weights, axis=-1, keepdims=True)
            probs = weights * (1.0 / mass)
            probs_low = probs.astype(jnp.bfloat16)
            mixed = jnp.dot(probs_low, values, preferred_element_type=jnp.float32)
            att_all[rows, :] = (gate_row * mixed).astype(jnp.bfloat16)
            gate_acc[...] += jnp.sum((cot * mixed).reshape(CHUNK // 8, 8, HEAD_DIM), axis=0)
            delta = jnp.sum(grad_heads.astype(jnp.float32) * mixed, axis=-1, keepdims=True)
            grad_probs = lax.dot_general(
                grad_heads, values, (((1,), (1,)), ((), ())), preferred_element_type=jnp.float32
            )
            grad_scores = (probs * (grad_probs - delta) * SCALE).astype(jnp.bfloat16)
            dq_all[rows, :] = jnp.dot(
                grad_scores, keys, preferred_element_type=jnp.float32
            ).astype(jnp.bfloat16)
            for part in range(PER_CHUNK):
                block = chunk * PER_CHUNK + part

                @pl.when(block != seq)
                def _():
                    for index in range(2):
                        row_copy(index, block).start()

                @pl.when(block == seq)
                def _():
                    for index, (source, sink) in enumerate(((att_all, att_ref), (dq_all, dq_ref))):
                        pltpu.make_async_copy(
                            source.at[rows_of(block)],
                            sink.at[0, 0, :, lanes_of(head)],
                            out_recv.at[index, head],
                        ).start()

            dk_acc[...] += lax.dot_general(
                grad_scores, queries, (((0,), (0,)), ((), ())), preferred_element_type=jnp.float32
            )
            dv_acc[...] += lax.dot_general(
                probs_low, grad_heads, (((0,), (0,)), ((), ())), preferred_element_type=jnp.float32
            )
            return carry

        lax.fori_loop(0, CHUNKS, one_chunk, 0)

        gate_in[pl.ds(clip, 1)] = gate_acc[...][None]

        def send_clip(step, carry):
            clip_copy(step).start()
            return carry

        lax.fori_loop(1, CLIPS, send_clip, 0)

        dk_all[...] = dk_acc[...].astype(jnp.bfloat16)
        dv_all[...] = dv_acc[...].astype(jnp.bfloat16)

        def send_columns(step, carry):
            block = (seq + step) % BLOCKS
            column_copy(0, block).start()
            column_copy(1, block).start()
            return carry

        lax.fori_loop(0, BLOCKS, send_columns, 0)

        def wait_clip(step, carry):
            other = (clip + step) % CLIPS
            pltpu.make_async_copy(gate_in.at[other], gate_in.at[other], clip_recv.at[other]).wait()
            return carry

        lax.fori_loop(1, CLIPS, wait_clip, 0)
        total = jnp.sum(jnp.sum(gate_in[...], axis=0), axis=0, keepdims=True)
        total = jnp.broadcast_to(total, (8, HEAD_DIM))
        gate_total[...] = total
        gate_heads[pl.ds(head, 1)] = total[None]

        def send_head(step, carry):
            head_copy(step).start()
            return carry

        lax.fori_loop(1, BLOCKS, send_head, 0)

    def wait_outputs(from_head, carry):
        for index, sink in enumerate((att_ref, dq_ref, dk_ref, dv_ref)):
            there = sink.at[0, 0, :, lanes_of(from_head)]
            pltpu.make_async_copy(there, there, out_recv.at[index, from_head]).wait()

        @pl.when(jnp.logical_or(from_head != head, jnp.logical_not(has_unit)))
        def _():
            there = gate_heads.at[from_head]
            pltpu.make_async_copy(there, there, head_recv.at[from_head]).wait()

        return carry

    lax.fori_loop(0, HEADS, wait_outputs, 0)
    for from_head in range(HEADS):
        gate_grad_ref[:, from_head * HEAD_DIM : (from_head + 1) * HEAD_DIM] = gate_heads[
            from_head, 0:1
        ]

    def wait_inputs_sent(step, carry):
        to_head, place = target(step, 1 - tower)
        for index, source in enumerate((key_ref, value_ref)):
            part = source.at[0, 0, :, lanes_of(to_head)]
            pltpu.make_async_copy(part, part, kv_send.at[index, to_head]).wait()
        to_head, place = target(step, tower)

        @pl.when(place != seq)
        def _():
            for index in range(2):
                query_copy(index, to_head, place).wait_send()

        return carry

    lax.fori_loop(0, HEADS, wait_inputs_sent, 0)

    @pl.when(has_unit)
    def _():
        def wait_sent(block, carry):
            for index in range(2):

                @pl.when(block != seq)
                def _():
                    row_copy(index, block).wait_send()

                column_copy(index, block).wait_send()
            return carry

        lax.fori_loop(0, BLOCKS, wait_sent, 0)

        def wait_clip_sent(step, carry):
            clip_copy(step).wait_send()
            return carry

        lax.fori_loop(1, CLIPS, wait_clip_sent, 0)

        def wait_head_sent(step, carry):
            head_copy(step).wait_send()
            return carry

        lax.fori_loop(1, BLOCKS, wait_head_sent, 0)


def local(query_proj, key_proj, value_proj, out_grad, gate_scale):
    whole = pl.BlockSpec(memory_space=pl.ANY)
    small = pl.BlockSpec(memory_space=pltpu.VMEM)
    big = jax.ShapeDtypeStruct((1, 1, ROWS, D), jnp.bfloat16)
    unit_rows = pltpu.VMEM((TOKENS, HEAD_DIM), jnp.bfloat16)
    unit_sums = pltpu.VMEM((TOKENS, HEAD_DIM), jnp.float32)
    gate_tile = pltpu.VMEM((8, HEAD_DIM), jnp.float32)
    dma = pltpu.SemaphoreType.DMA
    return pl.pallas_call(
        kernel,
        out_shape=(big, big, big, big, jax.ShapeDtypeStruct((1, D), jnp.float32)),
        in_specs=[whole] * 4 + [small],
        out_specs=(whole, whole, whole, whole, small),
        scratch_shapes=[
            unit_rows,
            unit_rows,
            unit_rows,
            unit_rows,
            unit_rows,
            unit_rows,
            unit_sums,
            unit_sums,
            unit_rows,
            unit_rows,
            gate_tile,
            pltpu.VMEM((CLIPS, 8, HEAD_DIM), jnp.float32),
            gate_tile,
            pltpu.VMEM((HEADS, 8, HEAD_DIM), jnp.float32),
            dma((2, HEADS)),
            dma((2, HEADS)),
            dma((BLOCKS,)),
            dma((BLOCKS,)),
            dma((BLOCKS,)),
            dma((BLOCKS,)),
            dma((2, BLOCKS)),
            dma((2, BLOCKS)),
            dma((4, HEADS)),
            dma((CLIPS,)),
            dma((CLIPS,)),
            dma((BLOCKS,)),
            dma((HEADS,)),
        ],
        compiler_params=pltpu.CompilerParams(
            collective_id=0, has_side_effects=True, vmem_limit_bytes=50 * 2**20
        ),
        cost_estimate=pl.CostEstimate(
            flops=12 * TOKENS * TOKENS * HEAD_DIM,
            bytes_accessed=16 * TOKENS * HEAD_DIM,
            transcendentals=TOKENS * TOKENS,
        ),
        name="heads_attention",
    )(query_proj, key_proj, value_proj, out_grad, gate_scale)


def solution(mesh):
    tokens = P("dp", "tower", "seq", None)
    gate = P("tower", None)
    return jax.shard_map(
        local,
        mesh=mesh,
        in_specs=(tokens, tokens, tokens, tokens, gate),
        out_specs=(tokens, tokens, tokens, tokens, gate),
        check_vma=False,
    )
```

```python
import math

import jax
import jax.numpy as jnp
from jax import lax
from jax.experimental import pallas as pl
from jax.experimental.pallas import tpu as pltpu
from jax.sharding import PartitionSpec as P

HEADS = 12
HEAD_DIM = 128
ROWS = 128
BLOCKS = 16
TOKENS = ROWS * BLOCKS
D = HEADS * HEAD_DIM
Z = 8
CLIPS = 8
CHUNK = 256
CHUNKS = TOKENS // CHUNK
PER_CHUNK = CHUNK // ROWS
SCALE = 1.0 / math.sqrt(HEAD_DIM)
EXP2_SCALE = SCALE * math.log2(math.e)
MESH = pl.DeviceIdType.MESH


def rows_of(block):
    return pl.ds(pl.multiple_of(block * ROWS, ROWS), ROWS)


def lanes_of(head):
    return pl.ds(pl.multiple_of(head * HEAD_DIM, HEAD_DIM), HEAD_DIM)


def kernel(
    query_ref,
    key_ref,
    value_ref,
    cot_ref,
    gate_ref,
    att_ref,
    dq_ref,
    dk_ref,
    dv_ref,
    gate_grad_ref,
    q_all,
    k_all,
    v_all,
    g_all,
    att_all,
    dq_all,
    dk_acc,
    dv_acc,
    dk_all,
    dv_all,
    gate_acc,
    gate_in,
    gate_total,
    gate_heads,
    kv_send,
    qg_send,
    k_recv,
    v_recv,
    q_recv,
    g_recv,
    rows_send,
    cols_send,
    out_recv,
    clip_send,
    clip_recv,
    head_send,
    head_recv,
):
    clip = lax.axis_index("dp")
    tower = lax.axis_index("tower")
    seq = lax.axis_index("seq")
    core = clip % 2
    x_hi = seq // Z
    z = seq % Z
    ring = (z + 2 * core + 16 - 2 * x_hi - tower) % Z
    has_unit = ring % 4 != 0
    slot = (ring // 4) * 3 + lax.max(ring % 4 - 1, 0)
    head = x_hi * 6 + slot

    def device(clip_to, tower_to, seq_to):
        return {"dp": clip_to, "tower": tower_to, "seq": seq_to}

    def peer_clip(step):
        other = (clip + step) % CLIPS
        other_z = (z + 2 * core + 16 - 2 * (other % 2)) % Z
        return other, x_hi * Z + other_z

    barrier = pltpu.get_barrier_semaphore()

    def greet(step, carry):
        place = (tower * BLOCKS + seq + step) % (2 * BLOCKS)
        pl.semaphore_signal(
            barrier,
            inc=1,
            device_id=device(clip, place // BLOCKS, place % BLOCKS),
            device_id_type=MESH,
        )
        return carry

    lax.fori_loop(1, 2 * BLOCKS, greet, 0)

    def greet_clip(step, carry):
        other, place = peer_clip(step)
        pl.semaphore_signal(
            barrier, inc=1, device_id=device(other, tower, place), device_id_type=MESH
        )
        return carry

    lax.fori_loop(1, CLIPS, greet_clip, 0)
    pl.semaphore_wait(barrier, 2 * BLOCKS - 1 + CLIPS - 1)

    def offset(turn):
        return ((turn + 1) // 2) * (2 * (turn % 2) - 1) * (1 - 2 * core)

    def offset_out(turn):
        turn = 7 - turn
        return ((turn + 1) // 2) * (2 * (turn % 2) - 1) * (1 - 2 * core)

    def target(step, tower_to):
        to_x = (x_hi + step) % 2
        to_z = (z + offset(step // 2) + Z) % Z
        to_ring = (to_z + 2 * core + 16 - 2 * to_x - tower_to) % Z
        to_head = to_x * 6 + (to_ring // 4) * 3 + lax.max(to_ring % 4 - 1, 0)
        return to_ring % 4 != 0, to_head, to_x * Z + to_z

    def send_kv(step, carry):
        there, to_head, place = target(step, 1 - tower)

        @pl.when(there)
        def _():
            for index, (source, sink, arrived) in enumerate(
                ((key_ref, k_all, k_recv), (value_ref, v_all, v_recv))
            ):
                pltpu.make_async_remote_copy(
                    src_ref=source.at[0, 0, :, lanes_of(to_head)],
                    dst_ref=sink.at[rows_of(seq)],
                    send_sem=kv_send.at[index, to_head],
                    recv_sem=arrived.at[seq],
                    device_id=device(clip, 1 - tower, place),
                    device_id_type=MESH,
                ).start()

        return carry

    lax.fori_loop(0, BLOCKS, send_kv, 0)

    def query_copy(index, to_head, place):
        source, sink, arrived = ((query_ref, q_all, q_recv), (cot_ref, g_all, g_recv))[index]
        return pltpu.make_async_remote_copy(
            src_ref=source.at[0, 0, :, lanes_of(to_head)],
            dst_ref=sink.at[rows_of(seq)],
            send_sem=qg_send.at[index, to_head],
            recv_sem=arrived.at[seq],
            device_id=device(clip, tower, place),
            device_id_type=MESH,
        )

    def send_qg(step, carry):
        there, to_head, place = target(step, tower)

        @pl.when(jnp.logical_and(there, place != seq))
        def _():
            for index in range(2):
                query_copy(index, to_head, place).start()

        @pl.when(jnp.logical_and(there, place == seq))
        def _():
            for source, sink, arrived in ((query_ref, q_all, q_recv), (cot_ref, g_all, g_recv)):
                pltpu.make_async_copy(
                    source.at[0, 0, :, lanes_of(to_head)],
                    sink.at[rows_of(seq)],
                    arrived.at[seq],
                ).start()

        return carry

    lax.fori_loop(0, BLOCKS, send_qg, 0)

    def row_copy(index, block):
        source, sink = ((att_all, att_ref), (dq_all, dq_ref))[index]
        return pltpu.make_async_remote_copy(
            src_ref=source.at[rows_of(block)],
            dst_ref=sink.at[0, 0, :, lanes_of(head)],
            send_sem=rows_send.at[index, block],
            recv_sem=out_recv.at[index, head],
            device_id=device(clip, tower, block),
            device_id_type=MESH,
        )

    def column_copy(index, block):
        source, sink = ((dk_all, dk_ref), (dv_all, dv_ref))[index]
        return pltpu.make_async_remote_copy(
            src_ref=source.at[rows_of(block)],
            dst_ref=sink.at[0, 0, :, lanes_of(head)],
            send_sem=cols_send.at[index, block],
            recv_sem=out_recv.at[2 + index, head],
            device_id=device(clip, 1 - tower, block),
            device_id_type=MESH,
        )

    def clip_copy(step):
        other, place = peer_clip(step)
        return pltpu.make_async_remote_copy(
            src_ref=gate_acc,
            dst_ref=gate_in.at[clip],
            send_sem=clip_send.at[step],
            recv_sem=clip_recv.at[clip],
            device_id=device(other, tower, place),
            device_id_type=MESH,
        )

    def head_copy(step):
        place = (seq + step) % BLOCKS
        return pltpu.make_async_remote_copy(
            src_ref=gate_total,
            dst_ref=gate_heads.at[head],
            send_sem=head_send.at[step],
            recv_sem=head_recv.at[head],
            device_id=device(clip, tower, place),
            device_id_type=MESH,
        )

    @pl.when(has_unit)
    def _():
        gate_row = gate_ref[:, lanes_of(head)]
        gate_acc[...] = jnp.zeros_like(gate_acc)
        dk_acc[...] = jnp.zeros_like(dk_acc)
        dv_acc[...] = jnp.zeros_like(dv_acc)

        def wait_kv(block, carry):
            pltpu.make_async_copy(
                k_all.at[rows_of(block)], k_all.at[rows_of(block)], k_recv.at[block]
            ).wait()
            pltpu.make_async_copy(
                v_all.at[rows_of(block)], v_all.at[rows_of(block)], v_recv.at[block]
            ).wait()
            return carry

        lax.fori_loop(0, BLOCKS, wait_kv, 0)

        def one_chunk(step, carry):
            chunk = (z - offset(step) + Z) % Z
            blocks = [part * Z + chunk for part in range(PER_CHUNK)]
            for block in blocks:
                pltpu.make_async_copy(
                    q_all.at[rows_of(block)], q_all.at[rows_of(block)], q_recv.at[block]
                ).wait()
                pltpu.make_async_copy(
                    g_all.at[rows_of(block)], g_all.at[rows_of(block)], g_recv.at[block]
                ).wait()

            def both(ref):
                return jnp.concatenate([ref[rows_of(block), :] for block in blocks], axis=0)

            def put(ref, values):
                for part, block in enumerate(blocks):
                    ref[rows_of(block), :] = values[part * ROWS : (part + 1) * ROWS]

            queries = both(q_all)
            keys = k_all[...]
            values = v_all[...]
            cot = both(g_all).astype(jnp.float32)
            grad_heads = (gate_row * cot).astype(jnp.bfloat16)
            scores = lax.dot_general(
                queries, keys, (((1,), (1,)), ((), ())), preferred_element_type=jnp.float32
            )
            row_top = jnp.max(scores, axis=-1, keepdims=True)
            weights = jnp.exp2((scores - row_top) * EXP2_SCALE)
            mass = jnp.sum(weights, axis=-1, keepdims=True)
            probs = weights * (1.0 / mass)
            probs_low = probs.astype(jnp.bfloat16)
            mixed = jnp.dot(probs_low, values, preferred_element_type=jnp.float32)
            put(att_all, (gate_row * mixed).astype(jnp.bfloat16))
            gate_acc[...] += jnp.sum((cot * mixed).reshape(CHUNK // 8, 8, HEAD_DIM), axis=0)
            delta = jnp.sum(grad_heads.astype(jnp.float32) * mixed, axis=-1, keepdims=True)
            grad_probs = lax.dot_general(
                grad_heads, values, (((1,), (1,)), ((), ())), preferred_element_type=jnp.float32
            )
            grad_scores = (probs * (grad_probs - delta) * SCALE).astype(jnp.bfloat16)
            query_grad = jnp.dot(grad_scores, keys, preferred_element_type=jnp.float32)
            put(dq_all, query_grad.astype(jnp.bfloat16))
            for block in blocks:

                @pl.when(block != seq)
                def _():
                    for index in range(2):
                        row_copy(index, block).start()

                @pl.when(block == seq)
                def _():
                    for index, (source, sink) in enumerate(((att_all, att_ref), (dq_all, dq_ref))):
                        pltpu.make_async_copy(
                            source.at[rows_of(block)],
                            sink.at[0, 0, :, lanes_of(head)],
                            out_recv.at[index, head],
                        ).start()

            dk_acc[...] += lax.dot_general(
                grad_scores, queries, (((0,), (0,)), ((), ())), preferred_element_type=jnp.float32
            )
            dv_acc[...] += lax.dot_general(
                probs_low, grad_heads, (((0,), (0,)), ((), ())), preferred_element_type=jnp.float32
            )
            return carry

        lax.fori_loop(0, CHUNKS, one_chunk, 0)

        gate_in[pl.ds(clip, 1)] = gate_acc[...][None]

        def send_clip(step, carry):
            clip_copy(step).start()
            return carry

        lax.fori_loop(1, CLIPS, send_clip, 0)

        dk_all[...] = dk_acc[...].astype(jnp.bfloat16)
        dv_all[...] = dv_acc[...].astype(jnp.bfloat16)

        def send_columns(index):
            def send_column(step, carry):
                block = ((x_hi + step) % 2) * Z + (z + offset_out(step // 2) + Z) % Z
                column_copy(index, block).start()
                return carry

            lax.fori_loop(0, BLOCKS, send_column, 0)

        send_columns(0)

        def wait_clip(step, carry):
            other = (clip + step) % CLIPS
            pltpu.make_async_copy(gate_in.at[other], gate_in.at[other], clip_recv.at[other]).wait()
            return carry

        lax.fori_loop(1, CLIPS, wait_clip, 0)
        total = jnp.sum(jnp.sum(gate_in[...], axis=0), axis=0, keepdims=True)
        total = jnp.broadcast_to(total, (8, HEAD_DIM))
        gate_total[...] = total
        gate_heads[pl.ds(head, 1)] = total[None]

        def send_head(step, carry):
            head_copy(step).start()
            return carry

        lax.fori_loop(1, BLOCKS, send_head, 0)
        send_columns(1)

    def wait_outputs(from_head, carry):
        for index, sink in enumerate((att_ref, dq_ref, dk_ref, dv_ref)):
            there = sink.at[0, 0, :, lanes_of(from_head)]
            pltpu.make_async_copy(there, there, out_recv.at[index, from_head]).wait()

        @pl.when(jnp.logical_or(from_head != head, jnp.logical_not(has_unit)))
        def _():
            there = gate_heads.at[from_head]
            pltpu.make_async_copy(there, there, head_recv.at[from_head]).wait()

        return carry

    lax.fori_loop(0, HEADS, wait_outputs, 0)
    for from_head in range(HEADS):
        gate_grad_ref[:, from_head * HEAD_DIM : (from_head + 1) * HEAD_DIM] = gate_heads[
            from_head, 0:1
        ]

    def wait_inputs_sent(step, carry):
        there, to_head, place = target(step, 1 - tower)

        @pl.when(there)
        def _():
            for index, source in enumerate((key_ref, value_ref)):
                part = source.at[0, 0, :, lanes_of(to_head)]
                pltpu.make_async_copy(part, part, kv_send.at[index, to_head]).wait()

        there, to_head, place = target(step, tower)

        @pl.when(jnp.logical_and(there, place != seq))
        def _():
            for index in range(2):
                query_copy(index, to_head, place).wait_send()

        return carry

    lax.fori_loop(0, BLOCKS, wait_inputs_sent, 0)

    @pl.when(has_unit)
    def _():
        def wait_sent(block, carry):
            for index in range(2):

                @pl.when(block != seq)
                def _():
                    row_copy(index, block).wait_send()

                column_copy(index, block).wait_send()
            return carry

        lax.fori_loop(0, BLOCKS, wait_sent, 0)

        def wait_clip_sent(step, carry):
            clip_copy(step).wait_send()
            return carry

        lax.fori_loop(1, CLIPS, wait_clip_sent, 0)

        def wait_head_sent(step, carry):
            head_copy(step).wait_send()
            return carry

        lax.fori_loop(1, BLOCKS, wait_head_sent, 0)


def hand_on(*refs):
    sources, sinks, held, arrived, left = refs[:5], refs[5:10], refs[10:15], refs[15], refs[16]
    first = [
        pltpu.make_async_copy(source, mid, arrived.at[index])
        for index, (source, mid) in enumerate(zip(sources, held))
    ]
    second = [
        pltpu.make_async_copy(mid, sink, left.at[index])
        for index, (mid, sink) in enumerate(zip(held, sinks))
    ]
    for copy in first:
        copy.start()
    for before, after in zip(first, second):
        before.wait()
        after.start()
    for copy in second:
        copy.wait()


def local(query_proj, key_proj, value_proj, out_grad, gate_scale):
    whole = pl.BlockSpec(memory_space=pltpu.HBM)
    some = pl.BlockSpec(memory_space=pl.ANY)
    small = pl.BlockSpec(memory_space=pltpu.VMEM)
    big = jax.ShapeDtypeStruct((1, 1, ROWS, D), jnp.bfloat16)
    unit_rows = pltpu.VMEM((TOKENS, HEAD_DIM), jnp.bfloat16)
    unit_sums = pltpu.VMEM((TOKENS, HEAD_DIM), jnp.float32)
    gate_tile = pltpu.VMEM((8, HEAD_DIM), jnp.float32)
    dma = pltpu.SemaphoreType.DMA
    results = pl.pallas_call(
        kernel,
        out_shape=(big, big, big, big, jax.ShapeDtypeStruct((1, D), jnp.float32)),
        in_specs=[whole] * 4 + [small],
        out_specs=(some, some, some, some, small),
        scratch_shapes=[
            unit_rows,
            unit_rows,
            unit_rows,
            unit_rows,
            unit_rows,
            unit_rows,
            unit_sums,
            unit_sums,
            unit_rows,
            unit_rows,
            gate_tile,
            pltpu.VMEM((CLIPS, 8, HEAD_DIM), jnp.float32),
            gate_tile,
            pltpu.VMEM((HEADS, 8, HEAD_DIM), jnp.float32),
            dma((2, HEADS)),
            dma((2, HEADS)),
            dma((BLOCKS,)),
            dma((BLOCKS,)),
            dma((BLOCKS,)),
            dma((BLOCKS,)),
            dma((2, BLOCKS)),
            dma((2, BLOCKS)),
            dma((4, HEADS)),
            dma((CLIPS,)),
            dma((CLIPS,)),
            dma((BLOCKS,)),
            dma((HEADS,)),
        ],
        compiler_params=pltpu.CompilerParams(
            collective_id=0, has_side_effects=True, vmem_limit_bytes=63 * 2**20
        ),
        cost_estimate=pl.CostEstimate(
            flops=12 * TOKENS * TOKENS * HEAD_DIM,
            bytes_accessed=16 * TOKENS * HEAD_DIM,
            transcendentals=TOKENS * TOKENS,
        ),
        name="heads_attention",
    )(query_proj, key_proj, value_proj, out_grad, gate_scale)
    return pl.pallas_call(
        hand_on,
        out_shape=tuple(jax.ShapeDtypeStruct(r.shape, r.dtype) for r in results),
        in_specs=[whole] * 5,
        out_specs=(whole,) * 5,
        scratch_shapes=[pltpu.VMEM(r.shape, r.dtype) for r in results] + [dma((5,))] * 2,
        name="hand_on",
    )(*results)


def solution(mesh):
    tokens = P("dp", "tower", "seq", None)
    gate = P("tower", None)
    return jax.shard_map(
        local,
        mesh=mesh,
        in_specs=(tokens, tokens, tokens, tokens, gate),
        out_specs=(tokens, tokens, tokens, tokens, gate),
        check_vma=False,
    )
```

```python
import math

import jax
import jax.numpy as jnp
from jax import lax
from jax.experimental import pallas as pl
from jax.experimental.pallas import tpu as pltpu
from jax.sharding import PartitionSpec as P

HEADS = 12
HEAD_DIM = 128
ROWS = 128
BLOCKS = 16
TOKENS = ROWS * BLOCKS
D = HEADS * HEAD_DIM
Z = 8
CLIPS = 8
UNITS = 3
CHUNK = 256
CHUNKS = TOKENS // CHUNK
PER_CHUNK = CHUNK // ROWS
SCALE = 1.0 / math.sqrt(HEAD_DIM)
EXP2_SCALE = SCALE * math.log2(math.e)
MESH = pl.DeviceIdType.MESH


def rows_of(block):
    return pl.ds(pl.multiple_of(block * ROWS, ROWS), ROWS)


def lanes_of(head):
    return pl.ds(pl.multiple_of(head * HEAD_DIM, HEAD_DIM), HEAD_DIM)


def kernel(
    query_ref,
    key_ref,
    value_ref,
    cot_ref,
    gate_ref,
    att_ref,
    dq_ref,
    dk_ref,
    dv_ref,
    gate_grad_ref,
    q_all,
    k_all,
    v_all,
    g_all,
    att_all,
    dq_all,
    dk_acc,
    dv_acc,
    dk_all,
    dv_all,
    gate_acc,
    gate_own,
    gate_in,
    gate_rows,
    kv_send,
    qg_send,
    k_recv,
    v_recv,
    q_recv,
    g_recv,
    rows_send,
    cols_send,
    out_recv,
    gate_send,
    unit_recv,
    clip_send,
    clip_recv,
    row_send,
    row_recv,
    final_send,
    final_recv,
    relay,
    relay_recv,
    relay_send,
):
    clip = lax.axis_index("dp")
    tower = lax.axis_index("tower")
    seq = lax.axis_index("seq")
    core = clip % 2
    x_hi = seq // Z
    z = seq % Z
    ring = (z + 2 * core + 16 - 2 * x_hi - tower) % Z
    has_unit = ring % 4 != 0
    slot = (ring // 4) * 3 + lax.max(ring % 4 - 1, 0)
    head = x_hi * 6 + slot
    idle_x = (z + 2 * core) % 4
    idle_hi = idle_x // 2
    unit = (2 * x_hi + tower - idle_x + 7) % 4

    def device(clip_to, tower_to, seq_to):
        return {"dp": clip_to, "tower": tower_to, "seq": seq_to}

    def row_in(step):
        other = (clip + step) % CLIPS
        return other, (z + 2 * core + 16 - 2 * (other % 2)) % Z

    barrier = pltpu.get_barrier_semaphore()

    def greet(step, carry):
        place = (tower * BLOCKS + seq + step) % (2 * BLOCKS)
        pl.semaphore_signal(
            barrier,
            inc=1,
            device_id=device(clip, place // BLOCKS, place % BLOCKS),
            device_id_type=MESH,
        )
        return carry

    lax.fori_loop(1, 2 * BLOCKS, greet, 0)

    @pl.when(jnp.logical_not(has_unit))
    def _():
        def greet_clip(step, carry):
            other, other_z = row_in(step)
            pl.semaphore_signal(
                barrier,
                inc=1,
                device_id=device(other, idle_x % 2, idle_hi * Z + other_z),
                device_id_type=MESH,
            )
            return carry

        lax.fori_loop(1, CLIPS, greet_clip, 0)
        pl.semaphore_wait(barrier, 2 * BLOCKS - 1 + CLIPS - 1)

    @pl.when(has_unit)
    def _():
        pl.semaphore_wait(barrier, 2 * BLOCKS - 1)

    def offset(turn):
        return ((turn + 1) // 2) * (2 * (turn % 2) - 1) * (1 - 2 * core)

    def offset_out(turn):
        turn = 7 - turn
        return ((turn + 1) // 2) * (2 * (turn % 2) - 1) * (1 - 2 * core)

    def target(step, tower_to):
        to_x = (x_hi + step) % 2
        to_z = (z + offset(step // 2) + Z) % Z
        to_ring = (to_z + 2 * core + 16 - 2 * to_x - tower_to) % Z
        to_head = to_x * 6 + (to_ring // 4) * 3 + lax.max(to_ring % 4 - 1, 0)
        return to_ring % 4 != 0, to_head, to_x * Z + to_z

    def send_kv(step, carry):
        there, to_head, place = target(step, 1 - tower)

        @pl.when(there)
        def _():
            for index, (source, sink, arrived) in enumerate(
                ((key_ref, k_all, k_recv), (value_ref, v_all, v_recv))
            ):
                pltpu.make_async_remote_copy(
                    src_ref=source.at[0, 0, :, lanes_of(to_head)],
                    dst_ref=sink.at[rows_of(seq)],
                    send_sem=kv_send.at[index, to_head],
                    recv_sem=arrived.at[seq],
                    device_id=device(clip, 1 - tower, place),
                    device_id_type=MESH,
                ).start()

        return carry

    lax.fori_loop(0, BLOCKS, send_kv, 0)

    def query_copy(index, to_head, place):
        source, sink, arrived = ((query_ref, q_all, q_recv), (cot_ref, g_all, g_recv))[index]
        return pltpu.make_async_remote_copy(
            src_ref=source.at[0, 0, :, lanes_of(to_head)],
            dst_ref=sink.at[rows_of(seq)],
            send_sem=qg_send.at[index, to_head],
            recv_sem=arrived.at[seq],
            device_id=device(clip, tower, place),
            device_id_type=MESH,
        )

    def send_qg(step, carry):
        there, to_head, place = target(step, tower)

        @pl.when(jnp.logical_and(there, place != seq))
        def _():
            for index in range(2):
                query_copy(index, to_head, place).start()

        @pl.when(jnp.logical_and(there, place == seq))
        def _():
            for source, sink, arrived in ((query_ref, q_all, q_recv), (cot_ref, g_all, g_recv)):
                pltpu.make_async_copy(
                    source.at[0, 0, :, lanes_of(to_head)],
                    sink.at[rows_of(seq)],
                    arrived.at[seq],
                ).start()

        return carry

    lax.fori_loop(0, BLOCKS, send_qg, 0)

    def row_copy(index, block):
        source, sink = ((att_all, att_ref), (dq_all, dq_ref))[index]
        return pltpu.make_async_remote_copy(
            src_ref=source.at[rows_of(block)],
            dst_ref=sink.at[0, 0, :, lanes_of(head)],
            send_sem=rows_send.at[index, block],
            recv_sem=out_recv.at[index, head],
            device_id=device(clip, tower, block),
            device_id_type=MESH,
        )

    def column_copy(index, block):
        source, sink = ((dk_all, dk_ref), (dv_all, dv_ref))[index]
        return pltpu.make_async_remote_copy(
            src_ref=source.at[rows_of(block)],
            dst_ref=sink.at[0, 0, :, lanes_of(head)],
            send_sem=cols_send.at[index, block],
            recv_sem=out_recv.at[2 + index, head],
            device_id=device(clip, 1 - tower, block),
            device_id_type=MESH,
        )

    def passed_on(place_z):
        return idle_hi * Z + place_z

    def relay_copy(index, place_z):
        block = passed_on(place_z)
        return pltpu.make_async_remote_copy(
            src_ref=(att_all, dk_all)[index].at[rows_of(block)],
            dst_ref=relay.at[index, unit, place_z],
            send_sem=(rows_send, cols_send)[index].at[0, block],
            recv_sem=relay_recv.at[index, unit, place_z],
            device_id=device(clip, idle_x % 2, passed_on(z)),
            device_id_type=MESH,
        )

    def forward_copy(index, from_unit, place_z):
        from_tower, from_head = unit_at(from_unit)
        to_tower = (from_tower + index) % 2
        return pltpu.make_async_remote_copy(
            src_ref=relay.at[index, from_unit, place_z],
            dst_ref=(att_ref, dk_ref)[index].at[0, 0, :, lanes_of(from_head)],
            send_sem=relay_send.at[index, from_unit, place_z],
            recv_sem=out_recv.at[2 * index, from_head],
            device_id=device(clip, to_tower, passed_on(place_z)),
            device_id_type=MESH,
        )

    gate_place = device(clip, idle_x % 2, passed_on(z))

    def unit_gate_copy():
        return pltpu.make_async_remote_copy(
            src_ref=gate_own,
            dst_ref=gate_in.at[clip, unit],
            send_sem=gate_send,
            recv_sem=unit_recv.at[unit],
            device_id=gate_place,
            device_id_type=MESH,
        )

    def clip_copy(step):
        other, other_z = row_in(step)
        return pltpu.make_async_remote_copy(
            src_ref=gate_in.at[clip],
            dst_ref=gate_in.at[clip],
            send_sem=clip_send.at[step],
            recv_sem=clip_recv.at[clip],
            device_id=device(other, idle_x % 2, idle_hi * Z + other_z),
            device_id_type=MESH,
        )

    def row_gate_copy(step):
        to_z = (z + step) % Z
        to_x = (to_z + 2 * core) % 4
        return pltpu.make_async_remote_copy(
            src_ref=gate_rows.at[z],
            dst_ref=gate_rows.at[z],
            send_sem=row_send.at[step],
            recv_sem=row_recv.at[z],
            device_id=device(clip, to_x % 2, (to_x // 2) * Z + to_z),
            device_id_type=MESH,
        )

    def final_gate_copy(to_unit):
        to_x = (idle_x + 1 + to_unit) % 4
        return pltpu.make_async_remote_copy(
            src_ref=gate_rows,
            dst_ref=gate_rows,
            send_sem=final_send.at[to_unit],
            recv_sem=final_recv,
            device_id=device(clip, to_x % 2, (to_x // 2) * Z + z),
            device_id_type=MESH,
        )

    def unit_at(from_unit):
        from_x = (idle_x + 1 + from_unit) % 4
        from_ring = (z + 2 * core + 16 - from_x) % Z
        from_head = (from_x // 2) * 6 + (from_ring // 4) * 3 + lax.max(from_ring % 4 - 1, 0)
        return from_x % 2, from_head

    @pl.when(has_unit)
    def _():
        gate_row = gate_ref[:, lanes_of(head)]
        gate_acc[...] = jnp.zeros_like(gate_acc)
        dk_acc[...] = jnp.zeros_like(dk_acc)
        dv_acc[...] = jnp.zeros_like(dv_acc)

        def wait_kv(block, carry):
            pltpu.make_async_copy(
                k_all.at[rows_of(block)], k_all.at[rows_of(block)], k_recv.at[block]
            ).wait()
            pltpu.make_async_copy(
                v_all.at[rows_of(block)], v_all.at[rows_of(block)], v_recv.at[block]
            ).wait()
            return carry

        lax.fori_loop(0, BLOCKS, wait_kv, 0)

        def one_chunk(step, carry):
            chunk = (z - offset(step) + Z) % Z
            blocks = [part * Z + chunk for part in range(PER_CHUNK)]
            for block in blocks:
                pltpu.make_async_copy(
                    q_all.at[rows_of(block)], q_all.at[rows_of(block)], q_recv.at[block]
                ).wait()
                pltpu.make_async_copy(
                    g_all.at[rows_of(block)], g_all.at[rows_of(block)], g_recv.at[block]
                ).wait()

            def both(ref):
                return jnp.concatenate([ref[rows_of(block), :] for block in blocks], axis=0)

            def put(ref, values):
                for part, block in enumerate(blocks):
                    ref[rows_of(block), :] = values[part * ROWS : (part + 1) * ROWS]

            queries = both(q_all)
            keys = k_all[...]
            values = v_all[...]
            cot = both(g_all).astype(jnp.float32)
            grad_heads = (gate_row * cot).astype(jnp.bfloat16)
            scores = lax.dot_general(
                queries, keys, (((1,), (1,)), ((), ())), preferred_element_type=jnp.float32
            )
            row_top = jnp.max(scores, axis=-1, keepdims=True)
            weights = jnp.exp2((scores - row_top) * EXP2_SCALE)
            mass = jnp.sum(weights, axis=-1, keepdims=True)
            probs = weights * (1.0 / mass)
            probs_low = probs.astype(jnp.bfloat16)
            mixed = jnp.dot(probs_low, values, preferred_element_type=jnp.float32)
            put(att_all, (gate_row * mixed).astype(jnp.bfloat16))
            gate_acc[...] += jnp.sum((cot * mixed).reshape(CHUNK // 8, 8, HEAD_DIM), axis=0)
            delta = jnp.sum(grad_heads.astype(jnp.float32) * mixed, axis=-1, keepdims=True)
            grad_probs = lax.dot_general(
                grad_heads, values, (((1,), (1,)), ((), ())), preferred_element_type=jnp.float32
            )
            grad_scores = (probs * (grad_probs - delta) * SCALE).astype(jnp.bfloat16)
            query_grad = jnp.dot(grad_scores, keys, preferred_element_type=jnp.float32)
            put(dq_all, query_grad.astype(jnp.bfloat16))
            for part, block in enumerate(blocks):
                passed = jnp.logical_and(part == idle_hi, chunk != z)

                @pl.when(passed)
                def _():
                    relay_copy(0, chunk).start()

                @pl.when(jnp.logical_and(block != seq, jnp.logical_not(passed)))
                def _():
                    row_copy(0, block).start()

                @pl.when(block != seq)
                def _():
                    row_copy(1, block).start()

                @pl.when(block == seq)
                def _():
                    for index, (source, sink) in enumerate(((att_all, att_ref), (dq_all, dq_ref))):
                        pltpu.make_async_copy(
                            source.at[rows_of(block)],
                            sink.at[0, 0, :, lanes_of(head)],
                            out_recv.at[index, head],
                        ).start()

            dk_acc[...] += lax.dot_general(
                grad_scores, queries, (((0,), (0,)), ((), ())), preferred_element_type=jnp.float32
            )
            dv_acc[...] += lax.dot_general(
                probs_low, grad_heads, (((0,), (0,)), ((), ())), preferred_element_type=jnp.float32
            )
            return carry

        lax.fori_loop(0, CHUNKS, one_chunk, 0)

        gate_own[...] = jnp.sum(gate_acc[...], axis=0, keepdims=True)

        unit_gate_copy().start()

        dk_all[...] = dk_acc[...].astype(jnp.bfloat16)
        dv_all[...] = dv_acc[...].astype(jnp.bfloat16)

        def send_relay(step, carry):
            relay_copy(1, (z + offset_out(step) + Z) % Z).start()
            return carry

        lax.fori_loop(0, Z - 1, send_relay, 0)

        def send_columns(index):
            def send_column(step, carry):
                place_z = (z + offset_out(step // 2) + Z) % Z
                place_x = (x_hi + step) % 2
                passed = jnp.logical_and(place_x == idle_hi, place_z != z)

                @pl.when(jnp.logical_or(index == 1, jnp.logical_not(passed)))
                def _():
                    column_copy(index, place_x * Z + place_z).start()

                return carry

            lax.fori_loop(0, BLOCKS, send_column, 0)

        send_columns(0)

        send_columns(1)

    @pl.when(jnp.logical_not(has_unit))
    def _():
        def forward(index, place_z):
            for from_unit in range(UNITS):
                held = relay.at[index, from_unit, place_z]
                pltpu.make_async_copy(
                    held, held, relay_recv.at[index, from_unit, place_z]
                ).wait()
                forward_copy(index, from_unit, place_z).start()

        def forward_rows(step, carry):
            forward(0, (z - offset(step) + Z) % Z)
            return carry

        lax.fori_loop(1, CHUNKS, forward_rows, 0)

        for from_unit in range(UNITS):
            there = gate_in.at[clip, from_unit]
            pltpu.make_async_copy(there, there, unit_recv.at[from_unit]).wait()

        def send_clip(step, carry):
            clip_copy(step).start()
            return carry

        lax.fori_loop(1, CLIPS, send_clip, 0)

        def forward_columns(step, carry):
            forward(1, (z + offset_out(step) + Z) % Z)
            return carry

        def wait_clip(step, carry):
            there = gate_in.at[(clip + step) % CLIPS]
            pltpu.make_async_copy(there, there, clip_recv.at[(clip + step) % CLIPS]).wait()
            return carry

        lax.fori_loop(1, CLIPS, wait_clip, 0)
        gate_rows[z] = jnp.sum(gate_in[...], axis=0)

        def send_row(step, carry):
            row_gate_copy(step).start()
            return carry

        lax.fori_loop(1, Z, send_row, 0)
        lax.fori_loop(0, Z - 1, forward_columns, 0)

        def wait_row(step, carry):
            there = gate_rows.at[(z + step) % Z]
            pltpu.make_async_copy(there, there, row_recv.at[(z + step) % Z]).wait()
            return carry

        lax.fori_loop(1, Z, wait_row, 0)
        for to_unit in range(UNITS):
            final_gate_copy(to_unit).start()

    def wait_outputs(from_head, carry):
        for index, sink in enumerate((att_ref, dq_ref, dk_ref, dv_ref)):
            there = sink.at[0, 0, :, lanes_of(from_head)]
            pltpu.make_async_copy(there, there, out_recv.at[index, from_head]).wait()

        return carry

    lax.fori_loop(0, HEADS, wait_outputs, 0)

    @pl.when(has_unit)
    def _():
        pltpu.make_async_copy(gate_rows, gate_rows, final_recv).wait()

    for from_head in range(HEADS):
        from_ring = from_head % 6 // 3 * 4 + from_head % 3 + 1
        from_z = (from_ring + 2 * (from_head // 6) + tower + 16 - 2 * core) % Z
        gate_grad_ref[:, from_head * HEAD_DIM : (from_head + 1) * HEAD_DIM] = gate_rows[
            from_z, 3 - from_ring % 4
        ]

    def wait_inputs_sent(step, carry):
        there, to_head, place = target(step, 1 - tower)

        @pl.when(there)
        def _():
            for index, source in enumerate((key_ref, value_ref)):
                part = source.at[0, 0, :, lanes_of(to_head)]
                pltpu.make_async_copy(part, part, kv_send.at[index, to_head]).wait()

        there, to_head, place = target(step, tower)

        @pl.when(jnp.logical_and(there, place != seq))
        def _():
            for index in range(2):
                query_copy(index, to_head, place).wait_send()

        return carry

    lax.fori_loop(0, BLOCKS, wait_inputs_sent, 0)

    @pl.when(has_unit)
    def _():
        def wait_sent(block, carry):
            for index in range(2):

                @pl.when(block != seq)
                def _():
                    row_copy(index, block).wait_send()

                column_copy(index, block).wait_send()
            return carry

        lax.fori_loop(0, BLOCKS, wait_sent, 0)

        unit_gate_copy().wait_send()

    @pl.when(jnp.logical_not(has_unit))
    def _():
        def wait_forwarded(step, carry):
            place_z = (z + step) % Z
            for index in range(2):
                for from_unit in range(UNITS):
                    forward_copy(index, from_unit, place_z).wait_send()
            return carry

        lax.fori_loop(1, Z, wait_forwarded, 0)

        def wait_gate_sent(step, carry):
            clip_copy(step).wait_send()
            row_gate_copy(step).wait_send()
            return carry

        lax.fori_loop(1, Z, wait_gate_sent, 0)
        for to_unit in range(UNITS):
            final_gate_copy(to_unit).wait_send()


def hand_on(*refs):
    sources, sinks, held, arrived, left = refs[:5], refs[5:10], refs[10:15], refs[15], refs[16]
    first = [
        pltpu.make_async_copy(source, mid, arrived.at[index])
        for index, (source, mid) in enumerate(zip(sources, held))
    ]
    second = [
        pltpu.make_async_copy(mid, sink, left.at[index])
        for index, (mid, sink) in enumerate(zip(held, sinks))
    ]
    for copy in first:
        copy.start()
    for before, after in zip(first, second):
        before.wait()
        after.start()
    for copy in second:
        copy.wait()


def local(query_proj, key_proj, value_proj, out_grad, gate_scale):
    whole = pl.BlockSpec(memory_space=pltpu.HBM)
    some = pl.BlockSpec(memory_space=pl.ANY)
    small = pl.BlockSpec(memory_space=pltpu.VMEM)
    big = jax.ShapeDtypeStruct((1, 1, ROWS, D), jnp.bfloat16)
    unit_rows = pltpu.VMEM((TOKENS, HEAD_DIM), jnp.bfloat16)
    unit_sums = pltpu.VMEM((TOKENS, HEAD_DIM), jnp.float32)
    dma = pltpu.SemaphoreType.DMA
    results = pl.pallas_call(
        kernel,
        out_shape=(big, big, big, big, jax.ShapeDtypeStruct((1, D), jnp.float32)),
        in_specs=[whole] * 4 + [small],
        out_specs=(some, some, some, some, small),
        scratch_shapes=[
            unit_rows,
            unit_rows,
            unit_rows,
            unit_rows,
            unit_rows,
            unit_rows,
            unit_sums,
            unit_sums,
            unit_rows,
            unit_rows,
            pltpu.VMEM((8, HEAD_DIM), jnp.float32),
            pltpu.VMEM((1, HEAD_DIM), jnp.float32),
            pltpu.VMEM((CLIPS, UNITS, 1, HEAD_DIM), jnp.float32),
            pltpu.VMEM((Z, UNITS, 1, HEAD_DIM), jnp.float32),
            dma((2, HEADS)),
            dma((2, HEADS)),
            dma((BLOCKS,)),
            dma((BLOCKS,)),
            dma((BLOCKS,)),
            dma((BLOCKS,)),
            dma((2, BLOCKS)),
            dma((2, BLOCKS)),
            dma((4, HEADS)),
            dma,
            dma((UNITS,)),
            dma((CLIPS,)),
            dma((CLIPS,)),
            dma((Z,)),
            dma((Z,)),
            dma((UNITS,)),
            dma,
            pltpu.VMEM((2, UNITS, Z, ROWS, HEAD_DIM), jnp.bfloat16),
            dma((2, UNITS, Z)),
            dma((2, UNITS, Z)),
        ],
        compiler_params=pltpu.CompilerParams(
            collective_id=0, has_side_effects=True, vmem_limit_bytes=63 * 2**20
        ),
        cost_estimate=pl.CostEstimate(
            flops=12 * TOKENS * TOKENS * HEAD_DIM,
            bytes_accessed=16 * TOKENS * HEAD_DIM,
            transcendentals=TOKENS * TOKENS,
        ),
        name="heads_attention",
    )(query_proj, key_proj, value_proj, out_grad, gate_scale)
    return pl.pallas_call(
        hand_on,
        out_shape=tuple(jax.ShapeDtypeStruct(r.shape, r.dtype) for r in results),
        in_specs=[whole] * 5,
        out_specs=(whole,) * 5,
        scratch_shapes=[pltpu.VMEM(r.shape, r.dtype) for r in results] + [dma((5,))] * 2,
        name="hand_on",
    )(*results)


def solution(mesh):
    tokens = P("dp", "tower", "seq", None)
    gate = P("tower", None)
    return jax.shard_map(
        local,
        mesh=mesh,
        in_specs=(tokens, tokens, tokens, tokens, gate),
        out_specs=(tokens, tokens, tokens, tokens, gate),
        check_vma=False,
    )
```

```python
import math

import jax
import jax.numpy as jnp
from jax import lax
from jax.experimental import pallas as pl
from jax.experimental.pallas import tpu as pltpu
from jax.sharding import PartitionSpec as P

HEADS = 12
HEAD_DIM = 128
ROWS = 128
BLOCKS = 16
TOKENS = ROWS * BLOCKS
D = HEADS * HEAD_DIM
Z = 8
CLIPS = 8
UNITS = 3
CHUNK = 256
CHUNKS = TOKENS // CHUNK
PER_CHUNK = CHUNK // ROWS
SCALE = 1.0 / math.sqrt(HEAD_DIM)
EXP2_SCALE = SCALE * math.log2(math.e)
MESH = pl.DeviceIdType.MESH


def rows_of(block):
    return pl.ds(pl.multiple_of(block * ROWS, ROWS), ROWS)


def lanes_of(head):
    return pl.ds(pl.multiple_of(head * HEAD_DIM, HEAD_DIM), HEAD_DIM)


def kernel(
    query_ref,
    key_ref,
    value_ref,
    cot_ref,
    gate_ref,
    att_ref,
    dq_ref,
    dk_ref,
    dv_ref,
    gate_grad_ref,
    gate_row_in,
    gate_row_out,
    gate_moved,
    q_all,
    k_all,
    v_all,
    g_all,
    att_all,
    dq_all,
    dk_acc,
    dv_acc,
    dk_all,
    dv_all,
    gate_acc,
    gate_own,
    gate_in,
    gate_rows,
    kv_send,
    qg_send,
    k_recv,
    v_recv,
    q_recv,
    g_recv,
    rows_send,
    cols_send,
    out_recv,
    gate_send,
    unit_recv,
    clip_send,
    clip_recv,
    row_send,
    row_recv,
    final_send,
    final_recv,
    relay,
    relay_recv,
    relay_send,
):
    clip = lax.axis_index("dp")
    tower = lax.axis_index("tower")
    seq = lax.axis_index("seq")
    core = clip % 2
    x_hi = seq // Z
    z = seq % Z
    ring = (z + 2 * core + 16 - 2 * x_hi - tower) % Z
    has_unit = ring % 4 != 0
    slot = (ring // 4) * 3 + lax.max(ring % 4 - 1, 0)
    head = x_hi * 6 + slot
    idle_x = (z + 2 * core) % 4
    idle_hi = idle_x // 2
    unit = (2 * x_hi + tower - idle_x + 7) % 4

    def device(clip_to, tower_to, seq_to):
        return {"dp": clip_to, "tower": tower_to, "seq": seq_to}

    def row_in(step):
        other = (clip + step) % CLIPS
        return other, (z + 2 * core + 16 - 2 * (other % 2)) % Z

    barrier = pltpu.get_barrier_semaphore()

    def greet(step, carry):
        place = (tower * BLOCKS + seq + step) % (2 * BLOCKS)
        pl.semaphore_signal(
            barrier,
            inc=1,
            device_id=device(clip, place // BLOCKS, place % BLOCKS),
            device_id_type=MESH,
        )
        return carry

    lax.fori_loop(1, 2 * BLOCKS, greet, 0, unroll=True)

    @pl.when(jnp.logical_not(has_unit))
    def _():
        def greet_clip(step, carry):
            other, other_z = row_in(step)
            pl.semaphore_signal(
                barrier,
                inc=1,
                device_id=device(other, idle_x % 2, idle_hi * Z + other_z),
                device_id_type=MESH,
            )
            return carry

        lax.fori_loop(1, CLIPS, greet_clip, 0)
        pl.semaphore_wait(barrier, 2 * BLOCKS - 1 + CLIPS - 1)

    @pl.when(has_unit)
    def _():
        pl.semaphore_wait(barrier, 2 * BLOCKS - 1)

    gate_here = pltpu.make_async_copy(gate_ref, gate_row_in, gate_moved.at[0])
    gate_here.start()

    def offset(turn):
        return ((turn + 1) // 2) * (2 * (turn % 2) - 1) * (1 - 2 * core)

    def offset_out(turn):
        turn = 7 - turn
        return ((turn + 1) // 2) * (2 * (turn % 2) - 1) * (1 - 2 * core)

    def target(step, tower_to, far=False):
        to_x = (x_hi + step) % 2
        to_z = (z + offset(7 - step // 2 if far else step // 2) + Z) % Z
        to_ring = (to_z + 2 * core + 16 - 2 * to_x - tower_to) % Z
        to_head = to_x * 6 + (to_ring // 4) * 3 + lax.max(to_ring % 4 - 1, 0)
        return to_ring % 4 != 0, to_head, to_x * Z + to_z

    def send_kv(step, carry):
        there, to_head, place = target(step, 1 - tower, True)

        @pl.when(there)
        def _():
            for index, (source, sink, arrived) in enumerate(
                ((key_ref, k_all, k_recv), (value_ref, v_all, v_recv))
            ):
                pltpu.make_async_remote_copy(
                    src_ref=source.at[0, 0, :, lanes_of(to_head)],
                    dst_ref=sink.at[rows_of(seq)],
                    send_sem=kv_send.at[index, to_head],
                    recv_sem=arrived.at[seq],
                    device_id=device(clip, 1 - tower, place),
                    device_id_type=MESH,
                ).start()

        return carry

    lax.fori_loop(0, BLOCKS, send_kv, 0)

    def query_copy(index, to_head, place):
        source, sink, arrived = ((query_ref, q_all, q_recv), (cot_ref, g_all, g_recv))[index]
        return pltpu.make_async_remote_copy(
            src_ref=source.at[0, 0, :, lanes_of(to_head)],
            dst_ref=sink.at[rows_of(seq)],
            send_sem=qg_send.at[index, to_head],
            recv_sem=arrived.at[seq],
            device_id=device(clip, tower, place),
            device_id_type=MESH,
        )

    def send_qg(step, carry):
        there, to_head, place = target(step, tower)

        @pl.when(jnp.logical_and(there, place != seq))
        def _():
            for index in range(2):
                query_copy(index, to_head, place).start()

        @pl.when(jnp.logical_and(there, place == seq))
        def _():
            for source, sink, arrived in ((query_ref, q_all, q_recv), (cot_ref, g_all, g_recv)):
                pltpu.make_async_copy(
                    source.at[0, 0, :, lanes_of(to_head)],
                    sink.at[rows_of(seq)],
                    arrived.at[seq],
                ).start()

        return carry

    lax.fori_loop(0, BLOCKS, send_qg, 0)

    def row_copy(index, block):
        source, sink = ((att_all, att_ref), (dq_all, dq_ref))[index]
        return pltpu.make_async_remote_copy(
            src_ref=source.at[rows_of(block)],
            dst_ref=sink.at[0, 0, :, lanes_of(head)],
            send_sem=rows_send.at[index, block],
            recv_sem=out_recv.at[index, head],
            device_id=device(clip, tower, block),
            device_id_type=MESH,
        )

    def column_copy(index, block):
        source, sink = ((dk_all, dk_ref), (dv_all, dv_ref))[index]
        return pltpu.make_async_remote_copy(
            src_ref=source.at[rows_of(block)],
            dst_ref=sink.at[0, 0, :, lanes_of(head)],
            send_sem=cols_send.at[index, block],
            recv_sem=out_recv.at[2 + index, head],
            device_id=device(clip, 1 - tower, block),
            device_id_type=MESH,
        )

    def passed_on(place_z):
        return idle_hi * Z + place_z

    def relay_copy(index, place_z):
        block = passed_on(place_z)
        return pltpu.make_async_remote_copy(
            src_ref=(att_all, dk_all)[index].at[rows_of(block)],
            dst_ref=relay.at[index, unit, place_z],
            send_sem=(rows_send, cols_send)[index].at[0, block],
            recv_sem=relay_recv.at[index, unit, place_z],
            device_id=device(clip, idle_x % 2, passed_on(z)),
            device_id_type=MESH,
        )

    def forward_copy(index, from_unit, place_z):
        from_tower, from_head = unit_at(from_unit)
        to_tower = (from_tower + index) % 2
        return pltpu.make_async_remote_copy(
            src_ref=relay.at[index, from_unit, place_z],
            dst_ref=(att_ref, dk_ref)[index].at[0, 0, :, lanes_of(from_head)],
            send_sem=relay_send.at[index, from_unit, place_z],
            recv_sem=out_recv.at[2 * index, from_head],
            device_id=device(clip, to_tower, passed_on(place_z)),
            device_id_type=MESH,
        )

    gate_place = device(clip, idle_x % 2, passed_on(z))

    def unit_gate_copy():
        return pltpu.make_async_remote_copy(
            src_ref=gate_own,
            dst_ref=gate_in.at[clip, unit],
            send_sem=gate_send,
            recv_sem=unit_recv.at[unit],
            device_id=gate_place,
            device_id_type=MESH,
        )

    def clip_copy(step):
        other, other_z = row_in(step)
        return pltpu.make_async_remote_copy(
            src_ref=gate_in.at[clip],
            dst_ref=gate_in.at[clip],
            send_sem=clip_send.at[step],
            recv_sem=clip_recv.at[clip],
            device_id=device(other, idle_x % 2, idle_hi * Z + other_z),
            device_id_type=MESH,
        )

    def row_gate_copy(step):
        to_z = (z + step) % Z
        to_x = (to_z + 2 * core) % 4
        return pltpu.make_async_remote_copy(
            src_ref=gate_rows.at[z],
            dst_ref=gate_rows.at[z],
            send_sem=row_send.at[step],
            recv_sem=row_recv.at[z],
            device_id=device(clip, to_x % 2, (to_x // 2) * Z + to_z),
            device_id_type=MESH,
        )

    def final_gate_copy(to_unit):
        to_x = (idle_x + 1 + to_unit) % 4
        return pltpu.make_async_remote_copy(
            src_ref=gate_rows,
            dst_ref=gate_rows,
            send_sem=final_send.at[to_unit],
            recv_sem=final_recv,
            device_id=device(clip, to_x % 2, (to_x // 2) * Z + z),
            device_id_type=MESH,
        )

    def unit_at(from_unit):
        from_x = (idle_x + 1 + from_unit) % 4
        from_ring = (z + 2 * core + 16 - from_x) % Z
        from_head = (from_x // 2) * 6 + (from_ring // 4) * 3 + lax.max(from_ring % 4 - 1, 0)
        return from_x % 2, from_head

    gate_here.wait()

    @pl.when(has_unit)
    def _():
        gate_row = gate_row_in[:, lanes_of(head)]
        gate_acc[...] = jnp.zeros_like(gate_acc)
        dk_acc[...] = jnp.zeros_like(dk_acc)
        dv_acc[...] = jnp.zeros_like(dv_acc)

        def wait_kv(block, carry):
            pltpu.make_async_copy(
                k_all.at[rows_of(block)], k_all.at[rows_of(block)], k_recv.at[block]
            ).wait()
            pltpu.make_async_copy(
                v_all.at[rows_of(block)], v_all.at[rows_of(block)], v_recv.at[block]
            ).wait()
            return carry

        lax.fori_loop(0, BLOCKS, wait_kv, 0)

        def one_chunk(step, carry):
            chunk = (z - offset(step) + Z) % Z
            blocks = [part * Z + chunk for part in range(PER_CHUNK)]
            for block in blocks:
                pltpu.make_async_copy(
                    q_all.at[rows_of(block)], q_all.at[rows_of(block)], q_recv.at[block]
                ).wait()
                pltpu.make_async_copy(
                    g_all.at[rows_of(block)], g_all.at[rows_of(block)], g_recv.at[block]
                ).wait()

            def both(ref):
                return jnp.concatenate([ref[rows_of(block), :] for block in blocks], axis=0)

            def put(ref, values):
                for part, block in enumerate(blocks):
                    ref[rows_of(block), :] = values[part * ROWS : (part + 1) * ROWS]

            queries = both(q_all)
            keys = k_all[...]
            values = v_all[...]
            cot = both(g_all).astype(jnp.float32)
            grad_heads = (gate_row * cot).astype(jnp.bfloat16)
            scores = lax.dot_general(
                queries, keys, (((1,), (1,)), ((), ())), preferred_element_type=jnp.float32
            )
            row_top = jnp.max(scores, axis=-1, keepdims=True)
            weights = jnp.exp2((scores - row_top) * EXP2_SCALE)
            mass = jnp.sum(weights, axis=-1, keepdims=True)
            probs = weights * (1.0 / mass)
            probs_low = probs.astype(jnp.bfloat16)
            mixed = jnp.dot(probs_low, values, preferred_element_type=jnp.float32)
            put(att_all, (gate_row * mixed).astype(jnp.bfloat16))
            gate_acc[...] += jnp.sum((cot * mixed).reshape(CHUNK // 8, 8, HEAD_DIM), axis=0)
            delta = jnp.sum(grad_heads.astype(jnp.float32) * mixed, axis=-1, keepdims=True)
            grad_probs = lax.dot_general(
                grad_heads, values, (((1,), (1,)), ((), ())), preferred_element_type=jnp.float32
            )
            grad_scores = (probs * (grad_probs - delta) * SCALE).astype(jnp.bfloat16)
            query_grad = jnp.dot(grad_scores, keys, preferred_element_type=jnp.float32)
            put(dq_all, query_grad.astype(jnp.bfloat16))
            for part, block in enumerate(blocks):
                passed = jnp.logical_and(part == idle_hi, chunk != z)

                @pl.when(passed)
                def _():
                    relay_copy(0, chunk).start()

                @pl.when(jnp.logical_and(block != seq, jnp.logical_not(passed)))
                def _():
                    row_copy(0, block).start()

                @pl.when(block != seq)
                def _():
                    row_copy(1, block).start()

                @pl.when(block == seq)
                def _():
                    for index, (source, sink) in enumerate(((att_all, att_ref), (dq_all, dq_ref))):
                        pltpu.make_async_copy(
                            source.at[rows_of(block)],
                            sink.at[0, 0, :, lanes_of(head)],
                            out_recv.at[index, head],
                        ).start()

            dk_acc[...] += lax.dot_general(
                grad_scores, queries, (((0,), (0,)), ((), ())), preferred_element_type=jnp.float32
            )
            dv_acc[...] += lax.dot_general(
                probs_low, grad_heads, (((0,), (0,)), ((), ())), preferred_element_type=jnp.float32
            )
            return carry

        lax.fori_loop(0, CHUNKS, one_chunk, 0)

        gate_own[...] = jnp.sum(gate_acc[...], axis=0, keepdims=True)

        unit_gate_copy().start()

        dk_all[...] = dk_acc[...].astype(jnp.bfloat16)
        dv_all[...] = dv_acc[...].astype(jnp.bfloat16)

        def send_relay(step, carry):
            relay_copy(1, (z + offset_out(step) + Z) % Z).start()
            return carry

        lax.fori_loop(0, Z - 1, send_relay, 0)

        def send_columns(index):
            def send_column(step, carry):
                place_z = (z + offset_out(step // 2) + Z) % Z
                place_x = (x_hi + step) % 2
                passed = jnp.logical_and(place_x == idle_hi, place_z != z)

                @pl.when(jnp.logical_or(index == 1, jnp.logical_not(passed)))
                def _():
                    column_copy(index, place_x * Z + place_z).start()

                return carry

            lax.fori_loop(0, BLOCKS, send_column, 0)

        send_columns(0)

        send_columns(1)

    @pl.when(jnp.logical_not(has_unit))
    def _():
        def forward(index, place_z):
            for from_unit in range(UNITS):
                held = relay.at[index, from_unit, place_z]
                pltpu.make_async_copy(
                    held, held, relay_recv.at[index, from_unit, place_z]
                ).wait()
                forward_copy(index, from_unit, place_z).start()

        def forward_rows(step, carry):
            forward(0, (z - offset(step) + Z) % Z)
            return carry

        lax.fori_loop(1, CHUNKS, forward_rows, 0)

        for from_unit in range(UNITS):
            there = gate_in.at[clip, from_unit]
            pltpu.make_async_copy(there, there, unit_recv.at[from_unit]).wait()

        def send_clip(step, carry):
            clip_copy(step).start()
            return carry

        lax.fori_loop(1, CLIPS, send_clip, 0)

        def forward_columns(step, carry):
            forward(1, (z + offset_out(step) + Z) % Z)
            return carry

        def wait_clip(step, carry):
            there = gate_in.at[(clip + step) % CLIPS]
            pltpu.make_async_copy(there, there, clip_recv.at[(clip + step) % CLIPS]).wait()
            return carry

        lax.fori_loop(1, CLIPS, wait_clip, 0)
        gate_rows[z] = jnp.sum(gate_in[...], axis=0)

        def send_row(step, carry):
            row_gate_copy(step).start()
            return carry

        lax.fori_loop(1, Z, send_row, 0)
        lax.fori_loop(0, Z - 1, forward_columns, 0)

        def wait_row(step, carry):
            there = gate_rows.at[(z + step) % Z]
            pltpu.make_async_copy(there, there, row_recv.at[(z + step) % Z]).wait()
            return carry

        lax.fori_loop(1, Z, wait_row, 0)
        for to_unit in range(UNITS):
            final_gate_copy(to_unit).start()

    @pl.when(has_unit)
    def _():
        pltpu.make_async_copy(gate_rows, gate_rows, final_recv).wait()

    for from_head in range(HEADS):
        from_ring = from_head % 6 // 3 * 4 + from_head % 3 + 1
        from_z = (from_ring + 2 * (from_head // 6) + tower + 16 - 2 * core) % Z
        gate_row_out[:, from_head * HEAD_DIM : (from_head + 1) * HEAD_DIM] = gate_rows[
            from_z, 3 - from_ring % 4
        ]
    gate_gone = pltpu.make_async_copy(gate_row_out, gate_grad_ref, gate_moved.at[1])
    gate_gone.start()

    def wait_outputs(from_head, carry):
        for index, sink in enumerate((att_ref, dq_ref, dk_ref, dv_ref)):
            there = sink.at[0, 0, :, lanes_of(from_head)]
            pltpu.make_async_copy(there, there, out_recv.at[index, from_head]).wait()

        return carry

    lax.fori_loop(0, HEADS, wait_outputs, 0)

    def wait_inputs_sent(step, carry):
        there, to_head, place = target(step, 1 - tower, True)

        @pl.when(there)
        def _():
            for index, source in enumerate((key_ref, value_ref)):
                part = source.at[0, 0, :, lanes_of(to_head)]
                pltpu.make_async_copy(part, part, kv_send.at[index, to_head]).wait()

        there, to_head, place = target(step, tower)

        @pl.when(jnp.logical_and(there, place != seq))
        def _():
            for index in range(2):
                query_copy(index, to_head, place).wait_send()

        return carry

    lax.fori_loop(0, BLOCKS, wait_inputs_sent, 0)

    @pl.when(has_unit)
    def _():
        def wait_sent(block, carry):
            for index in range(2):

                @pl.when(block != seq)
                def _():
                    row_copy(index, block).wait_send()

                column_copy(index, block).wait_send()
            return carry

        lax.fori_loop(0, BLOCKS, wait_sent, 0)

        unit_gate_copy().wait_send()

    @pl.when(jnp.logical_not(has_unit))
    def _():
        def wait_forwarded(step, carry):
            place_z = (z + step) % Z
            for index in range(2):
                for from_unit in range(UNITS):
                    forward_copy(index, from_unit, place_z).wait_send()
            return carry

        lax.fori_loop(1, Z, wait_forwarded, 0)

        def wait_gate_sent(step, carry):
            clip_copy(step).wait_send()
            row_gate_copy(step).wait_send()
            return carry

        lax.fori_loop(1, Z, wait_gate_sent, 0)
        for to_unit in range(UNITS):
            final_gate_copy(to_unit).wait_send()

    gate_gone.wait()


def hand_on(*refs):
    sources, sinks, held, arrived, left = refs[:5], refs[5:10], refs[10:15], refs[15], refs[16]
    first = [
        pltpu.make_async_copy(source, mid, arrived.at[index])
        for index, (source, mid) in enumerate(zip(sources, held))
    ]
    second = [
        pltpu.make_async_copy(mid, sink, left.at[index])
        for index, (mid, sink) in enumerate(zip(held, sinks))
    ]
    for copy in first:
        copy.start()
    for before, after in zip(first, second):
        before.wait()
        after.start()
    for copy in second:
        copy.wait()


def local(query_proj, key_proj, value_proj, out_grad, gate_scale):
    whole = pl.BlockSpec(memory_space=pl.ANY)
    big = jax.ShapeDtypeStruct((1, 1, ROWS, D), jnp.bfloat16)
    unit_rows = pltpu.VMEM((TOKENS, HEAD_DIM), jnp.bfloat16)
    unit_sums = pltpu.VMEM((TOKENS, HEAD_DIM), jnp.float32)
    dma = pltpu.SemaphoreType.DMA
    results = pl.pallas_call(
        kernel,
        out_shape=(big, big, big, big, jax.ShapeDtypeStruct((1, D), jnp.float32)),
        in_specs=[whole] * 5,
        out_specs=(whole,) * 5,
        scratch_shapes=[
            pltpu.VMEM((1, D), jnp.float32),
            pltpu.VMEM((1, D), jnp.float32),
            dma((2,)),
            unit_rows,
            unit_rows,
            unit_rows,
            unit_rows,
            unit_rows,
            unit_rows,
            unit_sums,
            unit_sums,
            unit_rows,
            unit_rows,
            pltpu.VMEM((8, HEAD_DIM), jnp.float32),
            pltpu.VMEM((1, HEAD_DIM), jnp.float32),
            pltpu.VMEM((CLIPS, UNITS, 1, HEAD_DIM), jnp.float32),
            pltpu.VMEM((Z, UNITS, 1, HEAD_DIM), jnp.float32),
            dma((2, HEADS)),
            dma((2, HEADS)),
            dma((BLOCKS,)),
            dma((BLOCKS,)),
            dma((BLOCKS,)),
            dma((BLOCKS,)),
            dma((2, BLOCKS)),
            dma((2, BLOCKS)),
            dma((4, HEADS)),
            dma,
            dma((UNITS,)),
            dma((CLIPS,)),
            dma((CLIPS,)),
            dma((Z,)),
            dma((Z,)),
            dma((UNITS,)),
            dma,
            pltpu.VMEM((2, UNITS, Z, ROWS, HEAD_DIM), jnp.bfloat16),
            dma((2, UNITS, Z)),
            dma((2, UNITS, Z)),
        ],
        compiler_params=pltpu.CompilerParams(
            collective_id=0, has_side_effects=True, vmem_limit_bytes=63 * 2**20
        ),
        cost_estimate=pl.CostEstimate(
            flops=12 * TOKENS * TOKENS * HEAD_DIM,
            bytes_accessed=16 * TOKENS * HEAD_DIM,
            transcendentals=TOKENS * TOKENS,
        ),
        name="heads_attention",
    )(query_proj, key_proj, value_proj, out_grad, gate_scale)
    return pl.pallas_call(
        hand_on,
        out_shape=tuple(jax.ShapeDtypeStruct(r.shape, r.dtype) for r in results),
        in_specs=[whole] * 5,
        out_specs=(whole,) * 5,
        scratch_shapes=[pltpu.VMEM(r.shape, r.dtype) for r in results] + [dma((5,))] * 2,
        name="hand_on",
    )(*results)


def solution(mesh):
    tokens = P("dp", "tower", "seq", None)
    gate = P("tower", None)
    return jax.shard_map(
        local,
        mesh=mesh,
        in_specs=(tokens, tokens, tokens, tokens, gate),
        out_specs=(tokens, tokens, tokens, tokens, gate),
        check_vma=False,
    )
```

```python
import math

import jax
import jax.numpy as jnp
from jax import lax
from jax.experimental import pallas as pl
from jax.experimental.pallas import tpu as pltpu
from jax.sharding import PartitionSpec as P

HEADS = 12
HEAD_DIM = 128
ROWS = 128
BLOCKS = 16
TOKENS = ROWS * BLOCKS
D = HEADS * HEAD_DIM
Z = 8
CLIPS = 8
UNITS = 3
CHUNK = 256
CHUNKS = TOKENS // CHUNK
PER_CHUNK = CHUNK // ROWS
SCALE = 1.0 / math.sqrt(HEAD_DIM)
EXP2_SCALE = SCALE * math.log2(math.e)
MESH = pl.DeviceIdType.MESH


def wait_for(ref, done):
    pltpu.make_async_copy(ref, ref, done).wait()


def rows_of(block):
    return pl.ds(pl.multiple_of(block * ROWS, ROWS), ROWS)


def lanes_of(head):
    return pl.ds(pl.multiple_of(head * HEAD_DIM, HEAD_DIM), HEAD_DIM)


def kernel(
    query_ref,
    key_ref,
    value_ref,
    cot_ref,
    gate_ref,
    att_ref,
    dq_ref,
    dk_ref,
    dv_ref,
    gate_grad_ref,
    gate_row_in,
    gate_row_out,
    gate_moved,
    q_all,
    k_all,
    v_all,
    g_all,
    att_all,
    dq_all,
    dk_acc,
    dv_acc,
    dk_all,
    dv_all,
    gate_acc,
    gate_own,
    gate_in,
    gate_rows,
    kv_send,
    qg_send,
    k_recv,
    v_recv,
    q_recv,
    g_recv,
    rows_send,
    cols_send,
    out_recv,
    gate_send,
    unit_recv,
    clip_send,
    clip_recv,
    row_send,
    row_recv,
    final_send,
    final_recv,
    relay,
    relay_recv,
    relay_send,
):
    clip = lax.axis_index("dp")
    tower = lax.axis_index("tower")
    seq = lax.axis_index("seq")
    core = clip % 2
    x_hi = seq // Z
    z = seq % Z
    ring = (z + 2 * core + 16 - 2 * x_hi - tower) % Z
    has_unit = ring % 4 != 0
    slot = (ring // 4) * 3 + lax.max(ring % 4 - 1, 0)
    head = x_hi * 6 + slot
    idle_x = (z + 2 * core) % 4
    idle_hi = idle_x // 2
    unit = (2 * x_hi + tower - idle_x + 7) % 4

    def device(clip_to, tower_to, seq_to):
        return {"dp": clip_to, "tower": tower_to, "seq": seq_to}

    def row_in(step):
        other = (clip + step) % CLIPS
        return other, (z + 2 * core + 16 - 2 * (other % 2)) % Z

    barrier = pltpu.get_barrier_semaphore()

    def greet(step, carry):
        place = (tower * BLOCKS + seq + step) % (2 * BLOCKS)
        pl.semaphore_signal(
            barrier,
            inc=1,
            device_id=device(clip, place // BLOCKS, place % BLOCKS),
            device_id_type=MESH,
        )
        return carry

    lax.fori_loop(1, 2 * BLOCKS, greet, 0, unroll=True)

    @pl.when(jnp.logical_not(has_unit))
    def _():
        def greet_clip(step, carry):
            other, other_z = row_in(step)
            pl.semaphore_signal(
                barrier,
                inc=1,
                device_id=device(other, idle_x % 2, idle_hi * Z + other_z),
                device_id_type=MESH,
            )
            return carry

        lax.fori_loop(1, CLIPS, greet_clip, 0)
        pl.semaphore_wait(barrier, 2 * BLOCKS - 1 + CLIPS - 1)

    @pl.when(has_unit)
    def _():
        pl.semaphore_wait(barrier, 2 * BLOCKS - 1)

    gate_here = pltpu.make_async_copy(gate_ref, gate_row_in, gate_moved.at[0])
    gate_here.start()

    def offset(turn):
        return ((turn + 1) // 2) * (2 * (turn % 2) - 1) * (1 - 2 * core)

    def offset_out(turn):
        turn = 7 - turn
        return ((turn + 1) // 2) * (2 * (turn % 2) - 1) * (1 - 2 * core)

    def target(step, tower_to, far=False):
        to_x = (x_hi + step) % 2
        to_z = (z + offset(7 - step // 2 if far else step // 2) + Z) % Z
        to_ring = (to_z + 2 * core + 16 - 2 * to_x - tower_to) % Z
        to_head = to_x * 6 + (to_ring // 4) * 3 + lax.max(to_ring % 4 - 1, 0)
        return to_ring % 4 != 0, to_head, to_x * Z + to_z

    def send_kv(step, carry):
        there, to_head, place = target(step, 1 - tower, True)

        @pl.when(there)
        def _():
            for index, (source, sink, arrived) in enumerate(
                ((key_ref, k_all, k_recv), (value_ref, v_all, v_recv))
            ):
                pltpu.make_async_remote_copy(
                    src_ref=source.at[0, 0, :, lanes_of(to_head)],
                    dst_ref=sink.at[rows_of(seq)],
                    send_sem=kv_send.at[index],
                    recv_sem=arrived,
                    device_id=device(clip, 1 - tower, place),
                    device_id_type=MESH,
                ).start()

        return carry

    lax.fori_loop(0, BLOCKS, send_kv, 0)

    def query_copy(index, to_head, place):
        source, sink, arrived = ((query_ref, q_all, q_recv), (cot_ref, g_all, g_recv))[index]
        return pltpu.make_async_remote_copy(
            src_ref=source.at[0, 0, :, lanes_of(to_head)],
            dst_ref=sink.at[rows_of(seq)],
            send_sem=qg_send.at[index],
            recv_sem=arrived.at[seq],
            device_id=device(clip, tower, place),
            device_id_type=MESH,
        )

    def send_qg(step, carry):
        there, to_head, place = target(step, tower)

        @pl.when(jnp.logical_and(there, place != seq))
        def _():
            for index in range(2):
                query_copy(index, to_head, place).start()

        @pl.when(jnp.logical_and(there, place == seq))
        def _():
            for source, sink, arrived in ((query_ref, q_all, q_recv), (cot_ref, g_all, g_recv)):
                pltpu.make_async_copy(
                    source.at[0, 0, :, lanes_of(to_head)],
                    sink.at[rows_of(seq)],
                    arrived.at[seq],
                ).start()

        return carry

    lax.fori_loop(0, BLOCKS, send_qg, 0)

    def row_copy(index, block):
        source, sink = ((att_all, att_ref), (dq_all, dq_ref))[index]
        return pltpu.make_async_remote_copy(
            src_ref=source.at[rows_of(block)],
            dst_ref=sink.at[0, 0, :, lanes_of(head)],
            send_sem=rows_send.at[index],
            recv_sem=out_recv.at[index],
            device_id=device(clip, tower, block),
            device_id_type=MESH,
        )

    def column_copy(index, block):
        source, sink = ((dk_all, dk_ref), (dv_all, dv_ref))[index]
        return pltpu.make_async_remote_copy(
            src_ref=source.at[rows_of(block)],
            dst_ref=sink.at[0, 0, :, lanes_of(head)],
            send_sem=cols_send.at[index],
            recv_sem=out_recv.at[2 + index],
            device_id=device(clip, 1 - tower, block),
            device_id_type=MESH,
        )

    def passed_on(place_z):
        return idle_hi * Z + place_z

    def relay_copy(index, place_z):
        block = passed_on(place_z)
        return pltpu.make_async_remote_copy(
            src_ref=(att_all, dk_all)[index].at[rows_of(block)],
            dst_ref=relay.at[index, unit, place_z],
            send_sem=(rows_send, cols_send)[index].at[0],
            recv_sem=relay_recv.at[index, unit, place_z],
            device_id=device(clip, idle_x % 2, passed_on(z)),
            device_id_type=MESH,
        )

    def forward_copy(index, from_unit, place_z):
        from_tower, from_head = unit_at(from_unit)
        to_tower = (from_tower + index) % 2
        return pltpu.make_async_remote_copy(
            src_ref=relay.at[index, from_unit, place_z],
            dst_ref=(att_ref, dk_ref)[index].at[0, 0, :, lanes_of(from_head)],
            send_sem=relay_send,
            recv_sem=out_recv.at[2 * index],
            device_id=device(clip, to_tower, passed_on(place_z)),
            device_id_type=MESH,
        )

    gate_place = device(clip, idle_x % 2, passed_on(z))

    def unit_gate_copy():
        return pltpu.make_async_remote_copy(
            src_ref=gate_own,
            dst_ref=gate_in.at[clip, unit],
            send_sem=gate_send,
            recv_sem=unit_recv.at[unit],
            device_id=gate_place,
            device_id_type=MESH,
        )

    def clip_copy(step):
        other, other_z = row_in(step)
        return pltpu.make_async_remote_copy(
            src_ref=gate_in.at[clip],
            dst_ref=gate_in.at[clip],
            send_sem=clip_send,
            recv_sem=clip_recv,
            device_id=device(other, idle_x % 2, idle_hi * Z + other_z),
            device_id_type=MESH,
        )

    def row_gate_copy(step):
        to_z = (z + step) % Z
        to_x = (to_z + 2 * core) % 4
        return pltpu.make_async_remote_copy(
            src_ref=gate_rows.at[z],
            dst_ref=gate_rows.at[z],
            send_sem=row_send,
            recv_sem=row_recv,
            device_id=device(clip, to_x % 2, (to_x // 2) * Z + to_z),
            device_id_type=MESH,
        )

    def final_gate_copy(to_unit):
        to_x = (idle_x + 1 + to_unit) % 4
        return pltpu.make_async_remote_copy(
            src_ref=gate_rows,
            dst_ref=gate_rows,
            send_sem=final_send.at[to_unit],
            recv_sem=final_recv,
            device_id=device(clip, to_x % 2, (to_x // 2) * Z + z),
            device_id_type=MESH,
        )

    def unit_at(from_unit):
        from_x = (idle_x + 1 + from_unit) % 4
        from_ring = (z + 2 * core + 16 - from_x) % Z
        from_head = (from_x // 2) * 6 + (from_ring // 4) * 3 + lax.max(from_ring % 4 - 1, 0)
        return from_x % 2, from_head

    gate_here.wait()

    @pl.when(has_unit)
    def _():
        gate_row = gate_row_in[:, lanes_of(head)]
        gate_acc[...] = jnp.zeros_like(gate_acc)
        dk_acc[...] = jnp.zeros_like(dk_acc)
        dv_acc[...] = jnp.zeros_like(dv_acc)

        wait_for(k_all, k_recv)
        wait_for(v_all, v_recv)

        def one_chunk(step, carry):
            chunk = (z - offset(step) + Z) % Z
            blocks = [part * Z + chunk for part in range(PER_CHUNK)]
            for block in blocks:
                pltpu.make_async_copy(
                    q_all.at[rows_of(block)], q_all.at[rows_of(block)], q_recv.at[block]
                ).wait()
                pltpu.make_async_copy(
                    g_all.at[rows_of(block)], g_all.at[rows_of(block)], g_recv.at[block]
                ).wait()

            def both(ref):
                return jnp.concatenate([ref[rows_of(block), :] for block in blocks], axis=0)

            def put(ref, values):
                for part, block in enumerate(blocks):
                    ref[rows_of(block), :] = values[part * ROWS : (part + 1) * ROWS]

            queries = both(q_all)
            keys = k_all[...]
            values = v_all[...]
            cot = both(g_all).astype(jnp.float32)
            grad_heads = (gate_row * cot).astype(jnp.bfloat16)
            scores = lax.dot_general(
                queries, keys, (((1,), (1,)), ((), ())), preferred_element_type=jnp.float32
            )
            row_top = jnp.max(scores, axis=-1, keepdims=True)
            weights = jnp.exp2((scores - row_top) * EXP2_SCALE)
            mass = jnp.sum(weights, axis=-1, keepdims=True)
            probs = weights * (1.0 / mass)
            probs_low = probs.astype(jnp.bfloat16)
            mixed = jnp.dot(probs_low, values, preferred_element_type=jnp.float32)
            put(att_all, (gate_row * mixed).astype(jnp.bfloat16))
            gate_acc[...] += jnp.sum((cot * mixed).reshape(CHUNK // 8, 8, HEAD_DIM), axis=0)
            delta = jnp.sum(grad_heads.astype(jnp.float32) * mixed, axis=-1, keepdims=True)
            grad_probs = lax.dot_general(
                grad_heads, values, (((1,), (1,)), ((), ())), preferred_element_type=jnp.float32
            )
            grad_scores = (probs * (grad_probs - delta) * SCALE).astype(jnp.bfloat16)
            query_grad = jnp.dot(grad_scores, keys, preferred_element_type=jnp.float32)
            put(dq_all, query_grad.astype(jnp.bfloat16))
            for part, block in enumerate(blocks):
                passed = jnp.logical_and(part == idle_hi, chunk != z)

                @pl.when(passed)
                def _():
                    relay_copy(0, chunk).start()

                @pl.when(jnp.logical_and(block != seq, jnp.logical_not(passed)))
                def _():
                    row_copy(0, block).start()

                @pl.when(block != seq)
                def _():
                    row_copy(1, block).start()

                @pl.when(block == seq)
                def _():
                    for index, (source, sink) in enumerate(((att_all, att_ref), (dq_all, dq_ref))):
                        pltpu.make_async_copy(
                            source.at[rows_of(block)],
                            sink.at[0, 0, :, lanes_of(head)],
                            out_recv.at[index],
                        ).start()

            dk_acc[...] += lax.dot_general(
                grad_scores, queries, (((0,), (0,)), ((), ())), preferred_element_type=jnp.float32
            )
            dv_acc[...] += lax.dot_general(
                probs_low, grad_heads, (((0,), (0,)), ((), ())), preferred_element_type=jnp.float32
            )
            return carry

        lax.fori_loop(0, CHUNKS, one_chunk, 0)

        gate_own[...] = jnp.sum(gate_acc[...], axis=0, keepdims=True)

        unit_gate_copy().start()

        dk_all[...] = dk_acc[...].astype(jnp.bfloat16)
        dv_all[...] = dv_acc[...].astype(jnp.bfloat16)

        def send_relay(step, carry):
            relay_copy(1, (z + offset_out(step) + Z) % Z).start()
            return carry

        lax.fori_loop(0, Z - 1, send_relay, 0)

        def send_columns(index):
            def send_column(step, carry):
                place_z = (z + offset_out(step // 2) + Z) % Z
                place_x = (x_hi + step) % 2
                passed = jnp.logical_and(place_x == idle_hi, place_z != z)

                @pl.when(jnp.logical_or(index == 1, jnp.logical_not(passed)))
                def _():
                    column_copy(index, place_x * Z + place_z).start()

                return carry

            lax.fori_loop(0, BLOCKS, send_column, 0)

        send_columns(0)

        send_columns(1)

    @pl.when(jnp.logical_not(has_unit))
    def _():
        def forward(index, place_z):
            for from_unit in range(UNITS):
                held = relay.at[index, from_unit, place_z]
                pltpu.make_async_copy(
                    held, held, relay_recv.at[index, from_unit, place_z]
                ).wait()
                forward_copy(index, from_unit, place_z).start()

        def forward_rows(step, carry):
            forward(0, (z - offset(step) + Z) % Z)
            return carry

        lax.fori_loop(1, CHUNKS, forward_rows, 0)

        for from_unit in range(UNITS):
            there = gate_in.at[clip, from_unit]
            pltpu.make_async_copy(there, there, unit_recv.at[from_unit]).wait()

        def send_clip(step, carry):
            clip_copy(step).start()
            return carry

        lax.fori_loop(1, CLIPS, send_clip, 0)

        def forward_columns(step, carry):
            forward(1, (z + offset_out(step) + Z) % Z)
            return carry

        wait_for(gate_in.at[pl.ds(0, CLIPS - 1)], clip_recv)
        gate_rows[z] = jnp.sum(gate_in[...], axis=0)

        def send_row(step, carry):
            row_gate_copy(step).start()
            return carry

        lax.fori_loop(1, Z, send_row, 0)
        lax.fori_loop(0, Z - 1, forward_columns, 0)

        wait_for(gate_rows.at[pl.ds(0, Z - 1)], row_recv)
        for to_unit in range(UNITS):
            final_gate_copy(to_unit).start()

    wait_for(key_ref, kv_send.at[0])
    wait_for(value_ref, kv_send.at[1])

    @pl.when(has_unit)
    def _():
        others = pl.ds(0, TOKENS - ROWS)
        rest = pl.ds(0, D - HEAD_DIM)
        for index in range(2):
            wait_for(query_ref.at[0, 0, :, rest], qg_send.at[index])
            wait_for(att_all.at[others], rows_send.at[index])
            wait_for(dk_all, cols_send.at[index])
        unit_gate_copy().wait_send()
        wait_for(gate_rows, final_recv)

    @pl.when(jnp.logical_not(has_unit))
    def _():
        for index in range(2):
            wait_for(query_ref, qg_send.at[index])
        wait_for(relay.at[:, :, pl.ds(0, Z - 1)], relay_send)
        wait_for(gate_in.at[pl.ds(0, CLIPS - 1)], clip_send)
        wait_for(gate_rows.at[pl.ds(0, Z - 1)], row_send)
        for to_unit in range(UNITS):
            final_gate_copy(to_unit).wait_send()

    for from_head in range(HEADS):
        from_ring = from_head % 6 // 3 * 4 + from_head % 3 + 1
        from_z = (from_ring + 2 * (from_head // 6) + tower + 16 - 2 * core) % Z
        gate_row_out[:, from_head * HEAD_DIM : (from_head + 1) * HEAD_DIM] = gate_rows[
            from_z, 3 - from_ring % 4
        ]
    gate_gone = pltpu.make_async_copy(gate_row_out, gate_grad_ref, gate_moved.at[1])
    gate_gone.start()
    for index, sink in enumerate((att_ref, dq_ref, dk_ref, dv_ref)):
        wait_for(sink, out_recv.at[index])
    gate_gone.wait()


def hand_on(*refs):
    sources, sinks, held, arrived, left = refs[:5], refs[5:10], refs[10:15], refs[15], refs[16]
    first = [
        pltpu.make_async_copy(source, mid, arrived.at[index])
        for index, (source, mid) in enumerate(zip(sources, held))
    ]
    second = [
        pltpu.make_async_copy(mid, sink, left.at[index])
        for index, (mid, sink) in enumerate(zip(held, sinks))
    ]
    for copy in first:
        copy.start()
    for before, after in zip(first, second):
        before.wait()
        after.start()
    for copy in second:
        copy.wait()


def local(query_proj, key_proj, value_proj, out_grad, gate_scale):
    whole = pl.BlockSpec(memory_space=pl.ANY)
    big = jax.ShapeDtypeStruct((1, 1, ROWS, D), jnp.bfloat16)
    unit_rows = pltpu.VMEM((TOKENS, HEAD_DIM), jnp.bfloat16)
    unit_sums = pltpu.VMEM((TOKENS, HEAD_DIM), jnp.float32)
    dma = pltpu.SemaphoreType.DMA
    results = pl.pallas_call(
        kernel,
        out_shape=(big, big, big, big, jax.ShapeDtypeStruct((1, D), jnp.float32)),
        in_specs=[whole] * 5,
        out_specs=(whole,) * 5,
        scratch_shapes=[
            pltpu.VMEM((1, D), jnp.float32),
            pltpu.VMEM((1, D), jnp.float32),
            dma((2,)),
            unit_rows,
            unit_rows,
            unit_rows,
            unit_rows,
            unit_rows,
            unit_rows,
            unit_sums,
            unit_sums,
            unit_rows,
            unit_rows,
            pltpu.VMEM((8, HEAD_DIM), jnp.float32),
            pltpu.VMEM((1, HEAD_DIM), jnp.float32),
            pltpu.VMEM((CLIPS, UNITS, 1, HEAD_DIM), jnp.float32),
            pltpu.VMEM((Z, UNITS, 1, HEAD_DIM), jnp.float32),
            dma((2,)),
            dma((2,)),
            dma,
            dma,
            dma((BLOCKS,)),
            dma((BLOCKS,)),
            dma((2,)),
            dma((2,)),
            dma((4,)),
            dma,
            dma((UNITS,)),
            dma,
            dma,
            dma,
            dma,
            dma((UNITS,)),
            dma,
            pltpu.VMEM((2, UNITS, Z, ROWS, HEAD_DIM), jnp.bfloat16),
            dma((2, UNITS, Z)),
            dma,
        ],
        compiler_params=pltpu.CompilerParams(
            collective_id=0, has_side_effects=True, vmem_limit_bytes=63 * 2**20
        ),
        cost_estimate=pl.CostEstimate(
            flops=12 * TOKENS * TOKENS * HEAD_DIM,
            bytes_accessed=16 * TOKENS * HEAD_DIM,
            transcendentals=TOKENS * TOKENS,
        ),
        name="heads_attention",
    )(query_proj, key_proj, value_proj, out_grad, gate_scale)
    return pl.pallas_call(
        hand_on,
        out_shape=tuple(jax.ShapeDtypeStruct(r.shape, r.dtype) for r in results),
        in_specs=[whole] * 5,
        out_specs=(whole,) * 5,
        scratch_shapes=[pltpu.VMEM(r.shape, r.dtype) for r in results] + [dma((5,))] * 2,
        name="hand_on",
    )(*results)


def solution(mesh):
    tokens = P("dp", "tower", "seq", None)
    gate = P("tower", None)
    return jax.shard_map(
        local,
        mesh=mesh,
        in_specs=(tokens, tokens, tokens, tokens, gate),
        out_specs=(tokens, tokens, tokens, tokens, gate),
        check_vma=False,
    )
```

```python
import math

import jax
import jax.numpy as jnp
from jax import lax
from jax.experimental import pallas as pl
from jax.experimental.pallas import tpu as pltpu
from jax.sharding import PartitionSpec as P

HEADS = 12
HEAD_DIM = 128
ROWS = 128
BLOCKS = 16
TOKENS = ROWS * BLOCKS
D = HEADS * HEAD_DIM
Z = 8
CLIPS = 8
UNITS = 3
CHUNK = 256
CHUNKS = TOKENS // CHUNK
PER_CHUNK = CHUNK // ROWS
SCALE = 1.0 / math.sqrt(HEAD_DIM)
EXP2_SCALE = SCALE * math.log2(math.e)
MESH = pl.DeviceIdType.MESH


def wait_for(ref, done):
    pltpu.make_async_copy(ref, ref, done).wait()


def rows_of(block):
    return pl.ds(pl.multiple_of(block * ROWS, ROWS), ROWS)


def lanes_of(head):
    return pl.ds(pl.multiple_of(head * HEAD_DIM, HEAD_DIM), HEAD_DIM)


def kernel(
    query_ref,
    key_ref,
    value_ref,
    cot_ref,
    gate_ref,
    att_ref,
    dq_ref,
    dk_ref,
    dv_ref,
    gate_grad_ref,
    gate_row_in,
    gate_row_out,
    gate_moved,
    q_all,
    k_all,
    v_all,
    g_all,
    att_all,
    dq_all,
    dk_acc,
    dv_acc,
    dk_all,
    dv_all,
    gate_acc,
    gate_own,
    gate_in,
    gate_rows,
    kv_send,
    qg_send,
    k_recv,
    v_recv,
    q_recv,
    g_recv,
    rows_send,
    cols_send,
    out_recv,
    gate_send,
    unit_recv,
    clip_send,
    clip_recv,
    row_send,
    row_recv,
    final_send,
    final_recv,
    relay,
    relay_recv,
    relay_send,
):
    clip = lax.axis_index("dp")
    tower = lax.axis_index("tower")
    seq = lax.axis_index("seq")
    core = clip % 2
    x_hi = seq // Z
    z = seq % Z
    ring = (z + 2 * core + 16 - 2 * x_hi - tower) % Z
    has_unit = ring % 4 != 0
    slot = (ring // 4) * 3 + lax.max(ring % 4 - 1, 0)
    head = x_hi * 6 + slot
    idle_x = (z + 2 * core) % 4
    idle_hi = idle_x // 2
    unit = (2 * x_hi + tower - idle_x + 7) % 4

    def device(clip_to, tower_to, seq_to):
        return {"dp": clip_to, "tower": tower_to, "seq": seq_to}

    def row_in(step):
        other = (clip + step) % CLIPS
        return other, (z + 2 * core + 16 - 2 * (other % 2)) % Z

    barrier = pltpu.get_barrier_semaphore()

    def greet(step, carry):
        place = (tower * BLOCKS + seq + step) % (2 * BLOCKS)
        pl.semaphore_signal(
            barrier,
            inc=1,
            device_id=device(clip, place // BLOCKS, place % BLOCKS),
            device_id_type=MESH,
        )
        return carry

    lax.fori_loop(1, 2 * BLOCKS, greet, 0, unroll=True)

    @pl.when(jnp.logical_not(has_unit))
    def _():
        def greet_clip(step, carry):
            other, other_z = row_in(step)
            pl.semaphore_signal(
                barrier,
                inc=1,
                device_id=device(other, idle_x % 2, idle_hi * Z + other_z),
                device_id_type=MESH,
            )
            return carry

        lax.fori_loop(1, CLIPS, greet_clip, 0)
        pl.semaphore_wait(barrier, 2 * BLOCKS - 1 + CLIPS - 1)

    @pl.when(has_unit)
    def _():
        pl.semaphore_wait(barrier, 2 * BLOCKS - 1)

    gate_here = pltpu.make_async_copy(gate_ref, gate_row_in, gate_moved.at[0])
    gate_here.start()

    def offset(turn):
        return ((turn + 1) // 2) * (2 * (turn % 2) - 1) * (1 - 2 * core)

    def offset_out(turn):
        turn = 7 - turn
        return ((turn + 1) // 2) * (2 * (turn % 2) - 1) * (1 - 2 * core)

    def target(step, tower_to, far=False):
        to_x = (x_hi + step) % 2
        to_z = (z + offset(7 - step // 2 if far else step // 2) + Z) % Z
        to_ring = (to_z + 2 * core + 16 - 2 * to_x - tower_to) % Z
        to_head = to_x * 6 + (to_ring // 4) * 3 + lax.max(to_ring % 4 - 1, 0)
        return to_ring % 4 != 0, to_head, to_x * Z + to_z

    def send_kv(step, carry):
        there, to_head, place = target(step, 1 - tower, True)

        @pl.when(there)
        def _():
            for index, (source, sink, arrived) in enumerate(
                ((key_ref, k_all, k_recv), (value_ref, v_all, v_recv))
            ):
                pltpu.make_async_remote_copy(
                    src_ref=source.at[0, 0, :, lanes_of(to_head)],
                    dst_ref=sink.at[rows_of(seq)],
                    send_sem=kv_send.at[index],
                    recv_sem=arrived,
                    device_id=device(clip, 1 - tower, place),
                    device_id_type=MESH,
                ).start()

        return carry

    lax.fori_loop(0, BLOCKS, send_kv, 0)

    def query_copy(index, to_head, place):
        source, sink, arrived = ((query_ref, q_all, q_recv), (cot_ref, g_all, g_recv))[index]
        return pltpu.make_async_remote_copy(
            src_ref=source.at[0, 0, :, lanes_of(to_head)],
            dst_ref=sink.at[rows_of(seq)],
            send_sem=qg_send.at[index],
            recv_sem=arrived.at[seq],
            device_id=device(clip, tower, place),
            device_id_type=MESH,
        )

    def send_qg(step, carry):
        there, to_head, place = target(step, tower)

        @pl.when(jnp.logical_and(there, place != seq))
        def _():
            for index in range(2):
                query_copy(index, to_head, place).start()

        @pl.when(jnp.logical_and(there, place == seq))
        def _():
            for source, sink, arrived in ((query_ref, q_all, q_recv), (cot_ref, g_all, g_recv)):
                pltpu.make_async_copy(
                    source.at[0, 0, :, lanes_of(to_head)],
                    sink.at[rows_of(seq)],
                    arrived.at[seq],
                ).start()

        return carry

    lax.fori_loop(0, BLOCKS, send_qg, 0)

    def row_copy(index, block):
        source, sink = ((att_all, att_ref), (dq_all, dq_ref))[index]
        return pltpu.make_async_remote_copy(
            src_ref=source.at[rows_of(block)],
            dst_ref=sink.at[0, 0, :, lanes_of(head)],
            send_sem=rows_send.at[index],
            recv_sem=out_recv.at[index],
            device_id=device(clip, tower, block),
            device_id_type=MESH,
        )

    def column_copy(index, block):
        source, sink = ((dk_all, dk_ref), (dv_all, dv_ref))[index]
        return pltpu.make_async_remote_copy(
            src_ref=source.at[rows_of(block)],
            dst_ref=sink.at[0, 0, :, lanes_of(head)],
            send_sem=cols_send.at[index],
            recv_sem=out_recv.at[2 + index],
            device_id=device(clip, 1 - tower, block),
            device_id_type=MESH,
        )

    def passed_on(place_z):
        return idle_hi * Z + place_z

    def relay_copy(index, place_z):
        block = passed_on(place_z)
        return pltpu.make_async_remote_copy(
            src_ref=(att_all, dk_all)[index].at[rows_of(block)],
            dst_ref=relay.at[index, unit, place_z],
            send_sem=(rows_send, cols_send)[index].at[0],
            recv_sem=relay_recv.at[index, unit, place_z],
            device_id=device(clip, idle_x % 2, passed_on(z)),
            device_id_type=MESH,
        )

    def forward_copy(index, from_unit, place_z):
        from_tower, from_head = unit_at(from_unit)
        to_tower = (from_tower + index) % 2
        return pltpu.make_async_remote_copy(
            src_ref=relay.at[index, from_unit, place_z],
            dst_ref=(att_ref, dk_ref)[index].at[0, 0, :, lanes_of(from_head)],
            send_sem=relay_send,
            recv_sem=out_recv.at[2 * index],
            device_id=device(clip, to_tower, passed_on(place_z)),
            device_id_type=MESH,
        )

    gate_place = device(clip, idle_x % 2, passed_on(z))

    def unit_gate_copy():
        return pltpu.make_async_remote_copy(
            src_ref=gate_own,
            dst_ref=gate_in.at[clip, unit],
            send_sem=gate_send,
            recv_sem=unit_recv.at[unit],
            device_id=gate_place,
            device_id_type=MESH,
        )

    def clip_copy(step):
        other, other_z = row_in(step)
        return pltpu.make_async_remote_copy(
            src_ref=gate_in.at[clip],
            dst_ref=gate_in.at[clip],
            send_sem=clip_send,
            recv_sem=clip_recv,
            device_id=device(other, idle_x % 2, idle_hi * Z + other_z),
            device_id_type=MESH,
        )

    def row_gate_copy(step):
        to_z = (z + step) % Z
        to_x = (to_z + 2 * core) % 4
        return pltpu.make_async_remote_copy(
            src_ref=gate_rows.at[z],
            dst_ref=gate_rows.at[z],
            send_sem=row_send,
            recv_sem=row_recv,
            device_id=device(clip, to_x % 2, (to_x // 2) * Z + to_z),
            device_id_type=MESH,
        )

    def final_gate_copy(to_unit):
        to_x = (idle_x + 1 + to_unit) % 4
        return pltpu.make_async_remote_copy(
            src_ref=gate_rows,
            dst_ref=gate_rows,
            send_sem=final_send.at[to_unit],
            recv_sem=final_recv,
            device_id=device(clip, to_x % 2, (to_x // 2) * Z + z),
            device_id_type=MESH,
        )

    def unit_at(from_unit):
        from_x = (idle_x + 1 + from_unit) % 4
        from_ring = (z + 2 * core + 16 - from_x) % Z
        from_head = (from_x // 2) * 6 + (from_ring // 4) * 3 + lax.max(from_ring % 4 - 1, 0)
        return from_x % 2, from_head

    gate_here.wait()

    @pl.when(has_unit)
    def _():
        gate_row = gate_row_in[:, lanes_of(head)]
        gate_acc[...] = jnp.zeros_like(gate_acc)
        dk_acc[...] = jnp.zeros_like(dk_acc)
        dv_acc[...] = jnp.zeros_like(dv_acc)

        wait_for(k_all, k_recv)
        wait_for(v_all, v_recv)

        def one_chunk(step, carry):
            chunk = (z - offset(step) + Z) % Z
            blocks = [part * Z + chunk for part in range(PER_CHUNK)]
            for block in blocks:
                pltpu.make_async_copy(
                    q_all.at[rows_of(block)], q_all.at[rows_of(block)], q_recv.at[block]
                ).wait()
                pltpu.make_async_copy(
                    g_all.at[rows_of(block)], g_all.at[rows_of(block)], g_recv.at[block]
                ).wait()

            def both(ref):
                return jnp.concatenate([ref[rows_of(block), :] for block in blocks], axis=0)

            def put(ref, values):
                for part, block in enumerate(blocks):
                    ref[rows_of(block), :] = values[part * ROWS : (part + 1) * ROWS]

            queries = both(q_all)
            keys = k_all[...]
            values = v_all[...]
            cot = both(g_all).astype(jnp.float32)
            grad_heads = (gate_row * cot).astype(jnp.bfloat16)
            scores = lax.dot_general(
                queries, keys, (((1,), (1,)), ((), ())), preferred_element_type=jnp.float32
            )
            row_top = jnp.max(scores, axis=-1, keepdims=True)
            weights = jnp.exp2((scores - row_top) * EXP2_SCALE)
            mass = jnp.sum(weights, axis=-1, keepdims=True)
            probs = weights * (1.0 / mass)
            probs_low = probs.astype(jnp.bfloat16)
            mixed = jnp.dot(probs_low, values, preferred_element_type=jnp.float32)
            put(att_all, (gate_row * mixed).astype(jnp.bfloat16))
            gate_acc[...] += jnp.sum((cot * mixed).reshape(CHUNK // 8, 8, HEAD_DIM), axis=0)
            delta = jnp.sum(grad_heads.astype(jnp.float32) * mixed, axis=-1, keepdims=True)
            grad_probs = lax.dot_general(
                grad_heads, values, (((1,), (1,)), ((), ())), preferred_element_type=jnp.float32
            )
            grad_scores = (probs * (grad_probs - delta)).astype(jnp.bfloat16)
            query_grad = jnp.dot(grad_scores, keys, preferred_element_type=jnp.float32)
            put(dq_all, (query_grad * SCALE).astype(jnp.bfloat16))
            for part, block in enumerate(blocks):
                passed = jnp.logical_and(part == idle_hi, chunk != z)

                @pl.when(passed)
                def _():
                    relay_copy(0, chunk).start()

                @pl.when(jnp.logical_and(block != seq, jnp.logical_not(passed)))
                def _():
                    row_copy(0, block).start()

                @pl.when(block != seq)
                def _():
                    row_copy(1, block).start()

                @pl.when(block == seq)
                def _():
                    for index, (source, sink) in enumerate(((att_all, att_ref), (dq_all, dq_ref))):
                        pltpu.make_async_copy(
                            source.at[rows_of(block)],
                            sink.at[0, 0, :, lanes_of(head)],
                            out_recv.at[index],
                        ).start()

            dk_acc[...] += lax.dot_general(
                grad_scores, queries, (((0,), (0,)), ((), ())), preferred_element_type=jnp.float32
            )
            dv_acc[...] += lax.dot_general(
                probs_low, grad_heads, (((0,), (0,)), ((), ())), preferred_element_type=jnp.float32
            )
            return carry

        lax.fori_loop(0, CHUNKS, one_chunk, 0)

        gate_own[...] = jnp.sum(gate_acc[...], axis=0, keepdims=True)

        unit_gate_copy().start()

        dk_all[...] = (dk_acc[...] * SCALE).astype(jnp.bfloat16)

        def send_relay(step, carry):
            relay_copy(1, (z + offset_out(step) + Z) % Z).start()
            return carry

        lax.fori_loop(0, Z - 1, send_relay, 0)

        def send_columns(index):
            def send_column(step, carry):
                place_z = (z + offset_out(step // 2) + Z) % Z
                place_x = (x_hi + step) % 2
                passed = jnp.logical_and(place_x == idle_hi, place_z != z)

                @pl.when(jnp.logical_or(index == 1, jnp.logical_not(passed)))
                def _():
                    column_copy(index, place_x * Z + place_z).start()

                return carry

            lax.fori_loop(0, BLOCKS, send_column, 0)

        send_columns(0)

        dv_all[...] = dv_acc[...].astype(jnp.bfloat16)
        send_columns(1)

    @pl.when(jnp.logical_not(has_unit))
    def _():
        def forward(index, place_z):
            for from_unit in range(UNITS):
                held = relay.at[index, from_unit, place_z]
                pltpu.make_async_copy(
                    held, held, relay_recv.at[index, from_unit, place_z]
                ).wait()
                forward_copy(index, from_unit, place_z).start()

        def forward_rows(step, carry):
            forward(0, (z - offset(step) + Z) % Z)
            return carry

        lax.fori_loop(1, CHUNKS, forward_rows, 0)

        for from_unit in range(UNITS):
            there = gate_in.at[clip, from_unit]
            pltpu.make_async_copy(there, there, unit_recv.at[from_unit]).wait()

        def send_clip(step, carry):
            clip_copy(step).start()
            return carry

        lax.fori_loop(1, CLIPS, send_clip, 0)

        def forward_columns(step, carry):
            forward(1, (z + offset_out(step) + Z) % Z)
            return carry

        wait_for(gate_in.at[pl.ds(0, CLIPS - 1)], clip_recv)
        gate_rows[z] = jnp.sum(gate_in[...], axis=0)

        def send_row(step, carry):
            row_gate_copy(step).start()
            return carry

        lax.fori_loop(1, Z, send_row, 0)
        lax.fori_loop(0, Z - 1, forward_columns, 0)

        wait_for(gate_rows.at[pl.ds(0, Z - 1)], row_recv)
        for to_unit in range(UNITS):
            final_gate_copy(to_unit).start()

    wait_for(key_ref, kv_send.at[0])
    wait_for(value_ref, kv_send.at[1])

    @pl.when(has_unit)
    def _():
        others = pl.ds(0, TOKENS - ROWS)
        rest = pl.ds(0, D - HEAD_DIM)
        for index in range(2):
            wait_for(query_ref.at[0, 0, :, rest], qg_send.at[index])
            wait_for(att_all.at[others], rows_send.at[index])
            wait_for(dk_all, cols_send.at[index])
        unit_gate_copy().wait_send()
        wait_for(gate_rows, final_recv)

    @pl.when(jnp.logical_not(has_unit))
    def _():
        for index in range(2):
            wait_for(query_ref, qg_send.at[index])
        wait_for(relay.at[:, :, pl.ds(0, Z - 1)], relay_send)
        wait_for(gate_in.at[pl.ds(0, CLIPS - 1)], clip_send)
        wait_for(gate_rows.at[pl.ds(0, Z - 1)], row_send)
        for to_unit in range(UNITS):
            final_gate_copy(to_unit).wait_send()

    for from_head in range(HEADS):
        from_ring = from_head % 6 // 3 * 4 + from_head % 3 + 1
        from_z = (from_ring + 2 * (from_head // 6) + tower + 16 - 2 * core) % Z
        gate_row_out[:, from_head * HEAD_DIM : (from_head + 1) * HEAD_DIM] = gate_rows[
            from_z, 3 - from_ring % 4
        ]
    gate_gone = pltpu.make_async_copy(gate_row_out, gate_grad_ref, gate_moved.at[1])
    gate_gone.start()
    for index, sink in enumerate((att_ref, dq_ref, dk_ref, dv_ref)):
        wait_for(sink, out_recv.at[index])
    gate_gone.wait()


def hand_on(*refs):
    sources, sinks, held, arrived, left = refs[:5], refs[5:10], refs[10:15], refs[15], refs[16]
    first = [
        pltpu.make_async_copy(source, mid, arrived.at[index])
        for index, (source, mid) in enumerate(zip(sources, held))
    ]
    second = [
        pltpu.make_async_copy(mid, sink, left.at[index])
        for index, (mid, sink) in enumerate(zip(held, sinks))
    ]
    for copy in first:
        copy.start()
    for before, after in zip(first, second):
        before.wait()
        after.start()
    for copy in second:
        copy.wait()


def local(query_proj, key_proj, value_proj, out_grad, gate_scale):
    whole = pl.BlockSpec(memory_space=pl.ANY)
    big = jax.ShapeDtypeStruct((1, 1, ROWS, D), jnp.bfloat16)
    unit_rows = pltpu.VMEM((TOKENS, HEAD_DIM), jnp.bfloat16)
    unit_sums = pltpu.VMEM((TOKENS, HEAD_DIM), jnp.float32)
    dma = pltpu.SemaphoreType.DMA
    results = pl.pallas_call(
        kernel,
        out_shape=(big, big, big, big, jax.ShapeDtypeStruct((1, D), jnp.float32)),
        in_specs=[whole] * 5,
        out_specs=(whole,) * 5,
        scratch_shapes=[
            pltpu.VMEM((1, D), jnp.float32),
            pltpu.VMEM((1, D), jnp.float32),
            dma((2,)),
            unit_rows,
            unit_rows,
            unit_rows,
            unit_rows,
            unit_rows,
            unit_rows,
            unit_sums,
            unit_sums,
            unit_rows,
            unit_rows,
            pltpu.VMEM((8, HEAD_DIM), jnp.float32),
            pltpu.VMEM((1, HEAD_DIM), jnp.float32),
            pltpu.VMEM((CLIPS, UNITS, 1, HEAD_DIM), jnp.float32),
            pltpu.VMEM((Z, UNITS, 1, HEAD_DIM), jnp.float32),
            dma((2,)),
            dma((2,)),
            dma,
            dma,
            dma((BLOCKS,)),
            dma((BLOCKS,)),
            dma((2,)),
            dma((2,)),
            dma((4,)),
            dma,
            dma((UNITS,)),
            dma,
            dma,
            dma,
            dma,
            dma((UNITS,)),
            dma,
            pltpu.VMEM((2, UNITS, Z, ROWS, HEAD_DIM), jnp.bfloat16),
            dma((2, UNITS, Z)),
            dma,
        ],
        compiler_params=pltpu.CompilerParams(
            collective_id=0, has_side_effects=True, vmem_limit_bytes=63 * 2**20
        ),
        cost_estimate=pl.CostEstimate(
            flops=12 * TOKENS * TOKENS * HEAD_DIM,
            bytes_accessed=16 * TOKENS * HEAD_DIM,
            transcendentals=TOKENS * TOKENS,
        ),
        name="heads_attention",
    )(query_proj, key_proj, value_proj, out_grad, gate_scale)
    return pl.pallas_call(
        hand_on,
        out_shape=tuple(jax.ShapeDtypeStruct(r.shape, r.dtype) for r in results),
        in_specs=[whole] * 5,
        out_specs=(whole,) * 5,
        scratch_shapes=[pltpu.VMEM(r.shape, r.dtype) for r in results] + [dma((5,))] * 2,
        name="hand_on",
    )(*results)


def solution(mesh):
    tokens = P("dp", "tower", "seq", None)
    gate = P("tower", None)
    return jax.shard_map(
        local,
        mesh=mesh,
        in_specs=(tokens, tokens, tokens, tokens, gate),
        out_specs=(tokens, tokens, tokens, tokens, gate),
        check_vma=False,
    )
```

```python
import math

import jax
import jax.numpy as jnp
from jax import lax
from jax.experimental import pallas as pl
from jax.experimental.pallas import tpu as pltpu
from jax.sharding import PartitionSpec as P

HEADS = 12
HEAD_DIM = 128
ROWS = 128
BLOCKS = 16
TOKENS = ROWS * BLOCKS
D = HEADS * HEAD_DIM
Z = 8
CLIPS = 8
UNITS = 3
CHUNK = 256
CHUNKS = TOKENS // CHUNK
PER_CHUNK = CHUNK // ROWS
SCALE = 1.0 / math.sqrt(HEAD_DIM)
EXP2_SCALE = SCALE * math.log2(math.e)
MESH = pl.DeviceIdType.MESH


def wait_for(ref, done):
    pltpu.make_async_copy(ref, ref, done).wait()


def rows_of(block):
    return pl.ds(pl.multiple_of(block * ROWS, ROWS), ROWS)


def lanes_of(head):
    return pl.ds(pl.multiple_of(head * HEAD_DIM, HEAD_DIM), HEAD_DIM)


def kernel(
    query_ref,
    key_ref,
    value_ref,
    cot_ref,
    gate_ref,
    att_ref,
    dq_ref,
    dk_ref,
    dv_ref,
    gate_grad_ref,
    gate_row_in,
    gate_row_out,
    gate_moved,
    q_all,
    k_all,
    v_all,
    g_all,
    att_all,
    dq_all,
    dk_acc,
    dv_acc,
    dk_all,
    dv_all,
    gate_acc,
    gate_own,
    gate_in,
    gate_rows,
    kv_send,
    qg_send,
    k_recv,
    v_recv,
    q_recv,
    g_recv,
    rows_send,
    cols_send,
    out_recv,
    gate_send,
    unit_recv,
    clip_send,
    clip_recv,
    row_send,
    row_recv,
    final_send,
    final_recv,
    relay,
    relay_recv,
    relay_send,
):
    clip = lax.axis_index("dp")
    tower = lax.axis_index("tower")
    seq = lax.axis_index("seq")
    core = clip % 2
    x_hi = seq // Z
    z = seq % Z
    ring = (z + 2 * core + 16 - 2 * x_hi - tower) % Z
    has_unit = ring % 4 != 0
    slot = (ring // 4) * 3 + lax.max(ring % 4 - 1, 0)
    head = x_hi * 6 + slot
    idle_x = (z + 2 * core) % 4
    idle_hi = idle_x // 2
    unit = (2 * x_hi + tower - idle_x + 7) % 4

    def device(clip_to, tower_to, seq_to):
        return {"dp": clip_to, "tower": tower_to, "seq": seq_to}

    def row_in(step):
        other = (clip + step) % CLIPS
        return other, (z + 2 * core + 16 - 2 * (other % 2)) % Z

    barrier = pltpu.get_barrier_semaphore()

    def greet(step, carry):
        place = (tower * BLOCKS + seq + step) % (2 * BLOCKS)
        pl.semaphore_signal(
            barrier,
            inc=1,
            device_id=device(clip, place // BLOCKS, place % BLOCKS),
            device_id_type=MESH,
        )
        return carry

    lax.fori_loop(1, 2 * BLOCKS, greet, 0, unroll=True)

    @pl.when(jnp.logical_not(has_unit))
    def _():
        def greet_clip(step, carry):
            other, other_z = row_in(step)
            pl.semaphore_signal(
                barrier,
                inc=1,
                device_id=device(other, idle_x % 2, idle_hi * Z + other_z),
                device_id_type=MESH,
            )
            return carry

        lax.fori_loop(1, CLIPS, greet_clip, 0)
        pl.semaphore_wait(barrier, 2 * BLOCKS - 1 + CLIPS - 1)

    @pl.when(has_unit)
    def _():
        pl.semaphore_wait(barrier, 2 * BLOCKS - 1)

    gate_here = pltpu.make_async_copy(gate_ref, gate_row_in, gate_moved.at[0])
    gate_here.start()

    def offset(turn):
        return ((turn + 1) // 2) * (2 * (turn % 2) - 1) * (1 - 2 * core)

    def offset_out(turn):
        turn = 7 - turn
        return ((turn + 1) // 2) * (2 * (turn % 2) - 1) * (1 - 2 * core)

    def target(step, tower_to, far=False):
        to_x = (x_hi + step) % 2
        to_z = (z + offset(7 - step // 2 if far else step // 2) + Z) % Z
        to_ring = (to_z + 2 * core + 16 - 2 * to_x - tower_to) % Z
        to_head = to_x * 6 + (to_ring // 4) * 3 + lax.max(to_ring % 4 - 1, 0)
        return to_ring % 4 != 0, to_head, to_x * Z + to_z

    def send_kv(step, carry):
        there, to_head, place = target(step, 1 - tower, True)

        @pl.when(there)
        def _():
            for index, (source, sink, arrived) in enumerate(
                ((key_ref, k_all, k_recv), (value_ref, v_all, v_recv))
            ):
                pltpu.make_async_remote_copy(
                    src_ref=source.at[0, 0, :, lanes_of(to_head)],
                    dst_ref=sink.at[rows_of(seq)],
                    send_sem=kv_send.at[index],
                    recv_sem=arrived,
                    device_id=device(clip, 1 - tower, place),
                    device_id_type=MESH,
                ).start()

        return carry

    lax.fori_loop(0, BLOCKS, send_kv, 0)

    def query_copy(index, to_head, place):
        source, sink, arrived = ((query_ref, q_all, q_recv), (cot_ref, g_all, g_recv))[index]
        return pltpu.make_async_remote_copy(
            src_ref=source.at[0, 0, :, lanes_of(to_head)],
            dst_ref=sink.at[rows_of(seq)],
            send_sem=qg_send.at[index],
            recv_sem=arrived.at[seq],
            device_id=device(clip, tower, place),
            device_id_type=MESH,
        )

    def send_qg(step, carry):
        there, to_head, place = target(step, tower)

        @pl.when(jnp.logical_and(there, place != seq))
        def _():
            for index in range(2):
                query_copy(index, to_head, place).start()

        @pl.when(jnp.logical_and(there, place == seq))
        def _():
            for source, sink, arrived in ((query_ref, q_all, q_recv), (cot_ref, g_all, g_recv)):
                pltpu.make_async_copy(
                    source.at[0, 0, :, lanes_of(to_head)],
                    sink.at[rows_of(seq)],
                    arrived.at[seq],
                ).start()

        return carry

    lax.fori_loop(0, BLOCKS, send_qg, 0)

    def row_copy(index, block):
        source, sink = ((att_all, att_ref), (dq_all, dq_ref))[index]
        return pltpu.make_async_remote_copy(
            src_ref=source.at[rows_of(block)],
            dst_ref=sink.at[0, 0, :, lanes_of(head)],
            send_sem=rows_send.at[index],
            recv_sem=out_recv.at[index],
            device_id=device(clip, tower, block),
            device_id_type=MESH,
        )

    def column_copy(index, block):
        source, sink = ((dk_all, dk_ref), (dv_all, dv_ref))[index]
        return pltpu.make_async_remote_copy(
            src_ref=source.at[rows_of(block)],
            dst_ref=sink.at[0, 0, :, lanes_of(head)],
            send_sem=cols_send.at[index],
            recv_sem=out_recv.at[2 + index],
            device_id=device(clip, 1 - tower, block),
            device_id_type=MESH,
        )

    def passed_on(place_z):
        return idle_hi * Z + place_z

    def relay_copy(index, place_z):
        block = (1 - x_hi) * Z + place_z if index == 0 else passed_on(place_z)
        return pltpu.make_async_remote_copy(
            src_ref=(att_all, dk_all)[index].at[rows_of(block)],
            dst_ref=relay.at[index, unit, place_z],
            send_sem=(rows_send, cols_send)[index].at[0],
            recv_sem=relay_recv.at[index, unit, place_z],
            device_id=device(clip, idle_x % 2, passed_on(z)),
            device_id_type=MESH,
        )

    def forward_copy(index, from_unit, place_z):
        from_tower, from_head = unit_at(from_unit)
        to_tower = (from_tower + index) % 2
        from_hi = (idle_x + 1 + from_unit) % 4 // 2
        to_seq = (1 - from_hi) * Z + place_z if index == 0 else passed_on(place_z)
        return pltpu.make_async_remote_copy(
            src_ref=relay.at[index, from_unit, place_z],
            dst_ref=(att_ref, dk_ref)[index].at[0, 0, :, lanes_of(from_head)],
            send_sem=relay_send,
            recv_sem=out_recv.at[2 * index],
            device_id=device(clip, to_tower, to_seq),
            device_id_type=MESH,
        )

    gate_place = device(clip, idle_x % 2, passed_on(z))

    def unit_gate_copy():
        return pltpu.make_async_remote_copy(
            src_ref=gate_own,
            dst_ref=gate_in.at[clip, unit],
            send_sem=gate_send,
            recv_sem=unit_recv.at[unit],
            device_id=gate_place,
            device_id_type=MESH,
        )

    def clip_copy(step):
        other, other_z = row_in(step)
        return pltpu.make_async_remote_copy(
            src_ref=gate_in.at[clip],
            dst_ref=gate_in.at[clip],
            send_sem=clip_send,
            recv_sem=clip_recv,
            device_id=device(other, idle_x % 2, idle_hi * Z + other_z),
            device_id_type=MESH,
        )

    def row_gate_copy(step):
        to_z = (z + step) % Z
        to_x = (to_z + 2 * core) % 4
        return pltpu.make_async_remote_copy(
            src_ref=gate_rows.at[z],
            dst_ref=gate_rows.at[z],
            send_sem=row_send,
            recv_sem=row_recv,
            device_id=device(clip, to_x % 2, (to_x // 2) * Z + to_z),
            device_id_type=MESH,
        )

    def final_gate_copy(to_unit):
        to_x = (idle_x + 1 + to_unit) % 4
        return pltpu.make_async_remote_copy(
            src_ref=gate_rows,
            dst_ref=gate_rows,
            send_sem=final_send.at[to_unit],
            recv_sem=final_recv,
            device_id=device(clip, to_x % 2, (to_x // 2) * Z + z),
            device_id_type=MESH,
        )

    def unit_at(from_unit):
        from_x = (idle_x + 1 + from_unit) % 4
        from_ring = (z + 2 * core + 16 - from_x) % Z
        from_head = (from_x // 2) * 6 + (from_ring // 4) * 3 + lax.max(from_ring % 4 - 1, 0)
        return from_x % 2, from_head

    gate_here.wait()

    @pl.when(has_unit)
    def _():
        gate_row = gate_row_in[:, lanes_of(head)]
        gate_acc[...] = jnp.zeros_like(gate_acc)
        dk_acc[...] = jnp.zeros_like(dk_acc)
        dv_acc[...] = jnp.zeros_like(dv_acc)

        wait_for(k_all, k_recv)
        wait_for(v_all, v_recv)

        def one_chunk(step, carry):
            chunk = (z - offset(step) + Z) % Z
            blocks = [part * Z + chunk for part in range(PER_CHUNK)]
            for block in blocks:
                pltpu.make_async_copy(
                    q_all.at[rows_of(block)], q_all.at[rows_of(block)], q_recv.at[block]
                ).wait()
                pltpu.make_async_copy(
                    g_all.at[rows_of(block)], g_all.at[rows_of(block)], g_recv.at[block]
                ).wait()

            def both(ref):
                return jnp.concatenate([ref[rows_of(block), :] for block in blocks], axis=0)

            def put(ref, values):
                for part, block in enumerate(blocks):
                    ref[rows_of(block), :] = values[part * ROWS : (part + 1) * ROWS]

            queries = both(q_all)
            keys = k_all[...]
            values = v_all[...]
            cot = both(g_all).astype(jnp.float32)
            grad_heads = (gate_row * cot).astype(jnp.bfloat16)
            scores = lax.dot_general(
                queries, keys, (((1,), (1,)), ((), ())), preferred_element_type=jnp.float32
            )
            row_top = jnp.max(scores, axis=-1, keepdims=True)
            weights = jnp.exp2((scores - row_top) * EXP2_SCALE)
            mass = jnp.sum(weights, axis=-1, keepdims=True)
            probs = weights * (1.0 / mass)
            probs_low = probs.astype(jnp.bfloat16)
            mixed = jnp.dot(probs_low, values, preferred_element_type=jnp.float32)
            put(att_all, (gate_row * mixed).astype(jnp.bfloat16))
            gate_acc[...] += jnp.sum((cot * mixed).reshape(CHUNK // 8, 8, HEAD_DIM), axis=0)
            delta = jnp.sum(grad_heads.astype(jnp.float32) * mixed, axis=-1, keepdims=True)
            grad_probs = lax.dot_general(
                grad_heads, values, (((1,), (1,)), ((), ())), preferred_element_type=jnp.float32
            )
            grad_scores = (probs * (grad_probs - delta) * SCALE).astype(jnp.bfloat16)
            query_grad = jnp.dot(grad_scores, keys, preferred_element_type=jnp.float32)
            put(dq_all, query_grad.astype(jnp.bfloat16))
            for part, block in enumerate(blocks):
                passed = jnp.logical_and(part != x_hi, chunk != z)

                @pl.when(passed)
                def _():
                    relay_copy(0, chunk).start()

                @pl.when(jnp.logical_and(block != seq, jnp.logical_not(passed)))
                def _():
                    row_copy(0, block).start()

                @pl.when(block != seq)
                def _():
                    row_copy(1, block).start()

                @pl.when(block == seq)
                def _():
                    for index, (source, sink) in enumerate(((att_all, att_ref), (dq_all, dq_ref))):
                        pltpu.make_async_copy(
                            source.at[rows_of(block)],
                            sink.at[0, 0, :, lanes_of(head)],
                            out_recv.at[index],
                        ).start()

            dk_acc[...] += lax.dot_general(
                grad_scores, queries, (((0,), (0,)), ((), ())), preferred_element_type=jnp.float32
            )
            dv_acc[...] += lax.dot_general(
                probs_low, grad_heads, (((0,), (0,)), ((), ())), preferred_element_type=jnp.float32
            )
            return carry

        lax.fori_loop(0, CHUNKS, one_chunk, 0)

        gate_own[...] = jnp.sum(gate_acc[...], axis=0, keepdims=True)

        unit_gate_copy().start()

        dk_all[...] = dk_acc[...].astype(jnp.bfloat16)
        dv_all[...] = dv_acc[...].astype(jnp.bfloat16)

        def send_relay(step, carry):
            relay_copy(1, (z + offset_out(step) + Z) % Z).start()
            return carry

        lax.fori_loop(0, Z - 1, send_relay, 0)

        def send_columns(index):
            def send_column(step, carry):
                place_z = (z + offset_out(step // 2) + Z) % Z
                place_x = (x_hi + step) % 2
                passed = jnp.logical_and(place_x == idle_hi, place_z != z)

                @pl.when(jnp.logical_or(index == 1, jnp.logical_not(passed)))
                def _():
                    column_copy(index, place_x * Z + place_z).start()

                return carry

            lax.fori_loop(0, BLOCKS, send_column, 0)

        send_columns(0)

        send_columns(1)

    @pl.when(jnp.logical_not(has_unit))
    def _():
        def forward(index, place_z):
            for from_unit in range(UNITS):
                held = relay.at[index, from_unit, place_z]
                pltpu.make_async_copy(
                    held, held, relay_recv.at[index, from_unit, place_z]
                ).wait()
                forward_copy(index, from_unit, place_z).start()

        def forward_rows(step, carry):
            forward(0, (z - offset(step) + Z) % Z)
            return carry

        lax.fori_loop(1, CHUNKS, forward_rows, 0)

        for from_unit in range(UNITS):
            there = gate_in.at[clip, from_unit]
            pltpu.make_async_copy(there, there, unit_recv.at[from_unit]).wait()

        def send_clip(step, carry):
            clip_copy(step).start()
            return carry

        lax.fori_loop(1, CLIPS, send_clip, 0)

        def forward_columns(step, carry):
            forward(1, (z + offset_out(step) + Z) % Z)
            return carry

        wait_for(gate_in.at[pl.ds(0, CLIPS - 1)], clip_recv)
        gate_rows[z] = jnp.sum(gate_in[...], axis=0)

        def send_row(step, carry):
            row_gate_copy(step).start()
            return carry

        lax.fori_loop(1, Z, send_row, 0)
        lax.fori_loop(0, Z - 1, forward_columns, 0)

        wait_for(gate_rows.at[pl.ds(0, Z - 1)], row_recv)
        for to_unit in range(UNITS):
            final_gate_copy(to_unit).start()

    wait_for(key_ref, kv_send.at[0])
    wait_for(value_ref, kv_send.at[1])

    @pl.when(has_unit)
    def _():
        others = pl.ds(0, TOKENS - ROWS)
        rest = pl.ds(0, D - HEAD_DIM)
        for index in range(2):
            wait_for(query_ref.at[0, 0, :, rest], qg_send.at[index])
            wait_for(att_all.at[others], rows_send.at[index])
            wait_for(dk_all, cols_send.at[index])
        unit_gate_copy().wait_send()
        wait_for(gate_rows, final_recv)

    @pl.when(jnp.logical_not(has_unit))
    def _():
        for index in range(2):
            wait_for(query_ref, qg_send.at[index])
        wait_for(relay.at[:, :, pl.ds(0, Z - 1)], relay_send)
        wait_for(gate_in.at[pl.ds(0, CLIPS - 1)], clip_send)
        wait_for(gate_rows.at[pl.ds(0, Z - 1)], row_send)
        for to_unit in range(UNITS):
            final_gate_copy(to_unit).wait_send()

    for from_head in range(HEADS):
        from_ring = from_head % 6 // 3 * 4 + from_head % 3 + 1
        from_z = (from_ring + 2 * (from_head // 6) + tower + 16 - 2 * core) % Z
        gate_row_out[:, from_head * HEAD_DIM : (from_head + 1) * HEAD_DIM] = gate_rows[
            from_z, 3 - from_ring % 4
        ]
    gate_gone = pltpu.make_async_copy(gate_row_out, gate_grad_ref, gate_moved.at[1])
    gate_gone.start()
    for index, sink in enumerate((att_ref, dq_ref, dk_ref, dv_ref)):
        wait_for(sink, out_recv.at[index])
    gate_gone.wait()


def hand_on(*refs):
    sources, sinks, held, arrived, left = refs[:5], refs[5:10], refs[10:15], refs[15], refs[16]
    first = [
        pltpu.make_async_copy(source, mid, arrived.at[index])
        for index, (source, mid) in enumerate(zip(sources, held))
    ]
    second = [
        pltpu.make_async_copy(mid, sink, left.at[index])
        for index, (mid, sink) in enumerate(zip(held, sinks))
    ]
    for copy in first:
        copy.start()
    for before, after in zip(first, second):
        before.wait()
        after.start()
    for copy in second:
        copy.wait()


def local(query_proj, key_proj, value_proj, out_grad, gate_scale):
    whole = pl.BlockSpec(memory_space=pl.ANY)
    big = jax.ShapeDtypeStruct((1, 1, ROWS, D), jnp.bfloat16)
    unit_rows = pltpu.VMEM((TOKENS, HEAD_DIM), jnp.bfloat16)
    unit_sums = pltpu.VMEM((TOKENS, HEAD_DIM), jnp.float32)
    dma = pltpu.SemaphoreType.DMA
    results = pl.pallas_call(
        kernel,
        out_shape=(big, big, big, big, jax.ShapeDtypeStruct((1, D), jnp.float32)),
        in_specs=[whole] * 5,
        out_specs=(whole,) * 5,
        scratch_shapes=[
            pltpu.VMEM((1, D), jnp.float32),
            pltpu.VMEM((1, D), jnp.float32),
            dma((2,)),
            unit_rows,
            unit_rows,
            unit_rows,
            unit_rows,
            unit_rows,
            unit_rows,
            unit_sums,
            unit_sums,
            unit_rows,
            unit_rows,
            pltpu.VMEM((8, HEAD_DIM), jnp.float32),
            pltpu.VMEM((1, HEAD_DIM), jnp.float32),
            pltpu.VMEM((CLIPS, UNITS, 1, HEAD_DIM), jnp.float32),
            pltpu.VMEM((Z, UNITS, 1, HEAD_DIM), jnp.float32),
            dma((2,)),
            dma((2,)),
            dma,
            dma,
            dma((BLOCKS,)),
            dma((BLOCKS,)),
            dma((2,)),
            dma((2,)),
            dma((4,)),
            dma,
            dma((UNITS,)),
            dma,
            dma,
            dma,
            dma,
            dma((UNITS,)),
            dma,
            pltpu.VMEM((2, UNITS, Z, ROWS, HEAD_DIM), jnp.bfloat16),
            dma((2, UNITS, Z)),
            dma,
        ],
        compiler_params=pltpu.CompilerParams(
            collective_id=0, has_side_effects=True, vmem_limit_bytes=63 * 2**20
        ),
        cost_estimate=pl.CostEstimate(
            flops=12 * TOKENS * TOKENS * HEAD_DIM,
            bytes_accessed=16 * TOKENS * HEAD_DIM,
            transcendentals=TOKENS * TOKENS,
        ),
        name="heads_attention",
    )(query_proj, key_proj, value_proj, out_grad, gate_scale)
    return pl.pallas_call(
        hand_on,
        out_shape=tuple(jax.ShapeDtypeStruct(r.shape, r.dtype) for r in results),
        in_specs=[whole] * 5,
        out_specs=(whole,) * 5,
        scratch_shapes=[pltpu.VMEM(r.shape, r.dtype) for r in results] + [dma((5,))] * 2,
        name="hand_on",
    )(*results)


def solution(mesh):
    tokens = P("dp", "tower", "seq", None)
    gate = P("tower", None)
    return jax.shard_map(
        local,
        mesh=mesh,
        in_specs=(tokens, tokens, tokens, tokens, gate),
        out_specs=(tokens, tokens, tokens, tokens, gate),
        check_vma=False,
    )
```
